256 devices in a mesh: dp: 16 (over x_hi, y, core), tile: 16 (over x_lo, z).
Axes of the slice: x: 4 (x_hi: 2, x_lo: 2; x = x_hi * 2 + x_lo), y: 4, z: 8, core: 2. Of those that a mesh axis runs over, the one named last changes fastest.
Arguments:
- images: bfloat16 [16, 64, 128, 256], P('dp', 'tile'), may hold values from -6 to 6
- cotangent: bfloat16 [16, 64, 128, 256], P('dp', 'tile'), may hold values from -6 to 6
- weight_one: bfloat16 [576, 256], P('tile'), may hold values from -0.25 to 0.25
- weight_two: bfloat16 [576, 256], P('tile'), may hold values from -0.25 to 0.25
Outputs:
- block_out: bfloat16 [16, 64, 128, 256], P('dp', 'tile')
- image_grad: bfloat16 [16, 64, 128, 256], P('dp', 'tile')
- grad_one: float32 [576, 256], P('tile')
- grad_two: float32 [576, 256], P('tile')
The draws below stay inside these ranges and needn't reach their ends.
All inputs are finite; a program needn't handle non-finite values.
Results may differ from the reference program's by a relative error of at most 0.0034.
Values may be sent and summed in bfloat16 or wider, within the bound.
No kernel may reach another device: no remote copies, remote signals or barrier semaphores. Data moves between devices by JAX's collectives and lax.ppermute only.
A program may use at most 64 MiB of HBM per device.

```python
import math
import jax
import jax.numpy as jnp
from jax import lax

C = 256
CG = 64
IMG_W = 128
SECTIONS = 16
ROWS = 64


def strengthened(result, own_key, source, target, shards_of, factor):
    def block_of(dim):
        return (jnp.arange(result.shape[dim]) // (result.shape[dim] // shards_of)).reshape((-1,) + (1,) * (result.ndim - 1 - dim))

    one_side = jax.random.permutation(own_key, shards_of)[block_of(target)]
    other_side = (block_of(target) + shards_of // 2) % shards_of
    return jnp.where((block_of(source) == one_side) | (block_of(source) == other_side), factor * result, result)


def block_scale(own_key, shape, split, smallest, high):
    factor_of, own = 1.0, jax.random.fold_in(own_key, 6)
    for position, parts in split:
        draws = jnp.exp(jax.random.uniform(jax.random.fold_in(own, position), (parts,), jnp.float32, smallest / len(split), high / len(split)))
        factor_of = factor_of * jnp.repeat(draws, shape[position] // parts).reshape([-1 if axis == position else 1 for axis in range(len(shape))])
    return factor_of


def normal_values(own_key, shape, scale, most, split=(), dtype=jnp.bfloat16):
    array = scale * jax.random.normal(own_key, shape, jnp.float32)
    if split:
        array = array * block_scale(own_key, shape, split, -0.22, 0.18)
    return jnp.clip(array, -most, most).astype(dtype)


def noise_with(rng, extent, spread, bound, split, heavy, dtype=jnp.bfloat16):
    array = spread * jax.random.normal(rng, extent, jnp.float32)
    if split:
        array = array * block_scale(rng, extent, split, -0.22, 0.18)
    return jnp.clip(strengthened(array, jax.random.fold_in(rng, 3), *heavy), -bound, bound).astype(dtype)


def setup_inputs(seed: int = 0) -> dict:
    key_of = jax.random.split(jax.random.key(seed), 5)
    return {
        "images": normal_values(key_of[0], (SECTIONS, ROWS, IMG_W, C), 1.0, 6.0, ((0, 16), (1, 16))),
        "cotangent": noise_with(key_of[1], (SECTIONS, ROWS, IMG_W, C), 1.0, 6.0, ((0, 16), (1, 16)), (1, 3, 16, 2.0)),
        "weight_one": normal_values(key_of[2], (9 * CG, C), (9 * CG) ** -0.5, 0.25, ((0, 16),)),
        "weight_two": normal_values(key_of[3], (9 * CG, C), (9 * CG) ** -0.5, 0.25, ((0, 16),)),
    }


def pad_both(field):
    return jnp.pad(field, ((1, 1), (1, 1), (0, 0)))

def conv_fwd(padded, weight, rows, cols):
    width = weight.shape[0] // 9
    groups = weight.shape[1] // width
    taps = weight.astype(jnp.float32).reshape(9, width, groups, width)
    total = jnp.zeros((rows, cols, groups, width), jnp.float32)
    for tap in range(9):
        row_off, col_off = divmod(tap, 3)
        patch = padded[row_off:row_off + rows, col_off:col_off + cols, :].astype(jnp.float32)
        patch = patch.reshape(rows, cols, groups, width)
        total = total + jnp.einsum('rwgi,igo->rwgo', patch, taps[tap])
    return total.reshape(rows, cols, groups * width)

def conv_back(padded, weight, rows, cols):
    width = weight.shape[0] // 9
    groups = weight.shape[1] // width
    taps = weight.astype(jnp.float32).reshape(9, width, groups, width)
    total = jnp.zeros((rows, cols, groups, width), jnp.float32)
    for tap in range(9):
        row_off, col_off = divmod(tap, 3)
        patch = padded[2 - row_off:2 - row_off + rows, 2 - col_off:2 - col_off + cols, :].astype(jnp.float32)
        patch = patch.reshape(rows, cols, groups, width)
        total = total + jnp.einsum('rwgo,igo->rwgi', patch, taps[tap])
    return total.reshape(rows, cols, groups * width)

def weight_grad(padded, upstream, width, rows, cols):
    groups = upstream.shape[-1] // width
    upper = upstream.astype(jnp.float32).reshape(rows, cols, groups, width)
    pieces = []
    for tap in range(9):
        row_off, col_off = divmod(tap, 3)
        patch = padded[row_off:row_off + rows, col_off:col_off + cols, :].astype(jnp.float32)
        patch = patch.reshape(rows, cols, groups, width)
        pieces.append(jnp.einsum('rwgi,rwgo->igo', patch, upper).reshape(width, groups * width))
    return jnp.concatenate(pieces, axis=0)

def silu_slope(pre):
    sig = jax.nn.sigmoid(pre)
    return sig * (1.0 + pre * (1.0 - sig))

def reference(images, cotangent, weight_one, weight_two):
    rows, cols = (images.shape[1], images.shape[2])
    width = weight_one.shape[0] // 9

    def one_section(carry, pair):
        image, upstream = pair
        xpad = pad_both(image)
        pre = conv_fwd(xpad, weight_one, rows, cols)
        act = jax.nn.silu(pre).astype(jnp.bfloat16)
        apad = pad_both(act)
        out = (image.astype(jnp.float32) + conv_fwd(apad, weight_two, rows, cols)).astype(jnp.bfloat16)
        dact = conv_back(pad_both(upstream), weight_two, rows, cols)
        dpre = (dact * silu_slope(pre)).astype(jnp.bfloat16)
        dimage = (upstream.astype(jnp.float32) + conv_back(pad_both(dpre), weight_one, rows, cols)).astype(jnp.bfloat16)
        sum_one = carry[0] + weight_grad(xpad, dpre, width, rows, cols)
        sum_two = carry[1] + weight_grad(apad, upstream, width, rows, cols)
        return ((sum_one, sum_two), (out, dimage))
    start = (jnp.zeros(weight_one.shape, jnp.float32), jnp.zeros(weight_two.shape, jnp.float32))
    sums, outputs = lax.scan(one_section, start, (images, cotangent))
    scale = 1.0 / math.sqrt(images.shape[0] * rows * cols)
    return (outputs[0], outputs[1], sums[0] * scale, sums[1] * scale)
```

```python
import math

import jax
import jax.numpy as jnp
from jax import lax
from jax.experimental import pallas as pl
from jax.experimental.pallas import tpu as pltpu
from jax.sharding import PartitionSpec as P

F32 = jnp.float32
BF16 = jnp.bfloat16


def dot(lhs, rhs, contract):
    return lax.dot_general(lhs, rhs, ((contract[:1], contract[1:]), ((), ())), preferred_element_type=F32)


def block_body(
    place, images, cotangent, above, below, mine, other,
    out, image_grad, keep, send,
    rows_one, rows_two, down_one, down_two, across_one, across_two,
    x_shifts, g_shifts, act_shifts, dpre_shifts, pre, dact, sum_one, sum_two,
):
    rows, cols, width = images.shape
    shards, shard_rows, _ = mine.shape
    depth = shards * shard_rows // 9
    groups = width // depth
    first_core = place[0] == 0
    for shard in range(shards):
        own, rest = mine[shard].astype(F32), other[shard].astype(F32)
        at = pl.ds(shard * shard_rows, shard_rows)
        rows_one[at, :] = jnp.where(first_core, own, rest)
        rows_two[at, :] = jnp.where(first_core, rest, own)

    line = lax.broadcasted_iota(jnp.int32, (width, width), 0) // depth
    lane = lax.broadcasted_iota(jnp.int32, (width, width), 1) // depth
    diagonal = line == lane
    for tap in range(9):
        a, b = divmod(tap, 3)
        for source, down, across in ((rows_one, down_one, across_one), (rows_two, down_two, across_two)):
            piece = source[tap * depth : (tap + 1) * depth, :]
            dense = jnp.where(diagonal, jnp.concatenate([piece] * groups, axis=0), 0.0).astype(BF16)
            down[tap * width : (tap + 1) * width, :] = dense
            across[a, :, (2 - b) * width : (3 - b) * width] = dense

    column = lax.broadcasted_iota(jnp.int32, (cols, width), 0)

    def put(shifts, row, value):
        wide = value.astype(F32)
        at = pl.ds(row * cols, cols)
        low = jnp.where(column == 0, 0.0, pltpu.roll(wide, 1, 0))
        high = jnp.where(column == cols - 1, 0.0, pltpu.roll(wide, cols - 1, 0))
        shifts[at, 0:width] = low.astype(BF16)
        shifts[at, width : 2 * width] = value.astype(BF16)
        shifts[at, 2 * width : 3 * width] = high.astype(BF16)

    for which, (shifts, block) in enumerate(((x_shifts, images), (g_shifts, cotangent))):
        for row in range(2):
            put(shifts, row, above[which, row])
            put(shifts, row + 2 + rows, below[which, row])
        for row in range(rows):
            put(shifts, row + 2, block[row])

    def conv(shifts, down, count):
        total = None
        for a in range(3):
            part = dot(shifts[a * cols : (a + count) * cols, :], down[a * 3 * width : (a + 1) * 3 * width, :], (1, 0))
            total = part if total is None else total + part
        return total

    def conv_back(shifts, across, count):
        total = None
        for a in range(3):
            part = dot(shifts[(2 - a) * cols : (2 - a + count) * cols, :], across[a], (1, 1))
            total = part if total is None else total + part
        return total

    pre[...] = conv(x_shifts, down_one, rows + 2)
    dact[...] = conv_back(g_shifts, across_two, rows + 2)
    for row in range(rows + 2):
        at = pl.ds(row * cols, cols)
        value = pre[at, :]
        sig = jax.nn.sigmoid(value)
        act = value * sig
        dpre = dact[at, :] * (sig * (1.0 + value * (1.0 - sig)))
        if row in (0, rows + 1):
            outside = place[1 if row == 0 else 2] == 1
            act = jnp.where(outside, 0.0, act)
            dpre = jnp.where(outside, 0.0, dpre)
        put(act_shifts, row, act)
        put(dpre_shifts, row, dpre)

    def weight_sum(field, upstream, total):
        turned = field.T
        group = lax.broadcasted_iota(jnp.int32, (depth, width), 1) // depth
        for a in range(3):
            dense = dot(turned[:, a * cols : (a + rows) * cols], upstream, (1, 0))
            for j in range(3):
                piece = jnp.zeros((depth, width), F32)
                for g in range(groups):
                    block = dense[g * depth : (g + 1) * depth, j * width : (j + 1) * width]
                    piece = jnp.where(group == g, block, piece)
                tap = 3 * a + 2 - j
                total[tap * depth : (tap + 1) * depth, :] = piece

    mid = slice(width, 2 * width)
    weight_sum(x_shifts[cols : (rows + 3) * cols, mid], dpre_shifts[cols : (rows + 1) * cols, :], sum_one)
    weight_sum(act_shifts[:, mid], g_shifts[2 * cols : (rows + 2) * cols, :], sum_two)
    for shard in range(shards):
        at = pl.ds(shard * shard_rows, shard_rows)
        one, two = sum_one[at, :], sum_two[at, :]
        keep[shard] = jnp.where(first_core, one, two)
        send[shard] = jnp.where(first_core, two, one).astype(BF16)

    total = conv(act_shifts, down_two, rows)
    back = conv_back(dpre_shifts, across_one, rows)
    for row in range(rows):
        at = slice(row * cols, (row + 1) * cols)
        out[row] = (images[row].astype(F32) + total[at, :]).astype(BF16)
        image_grad[row] = (cotangent[row].astype(F32) + back[at, :]).astype(BF16)


def block_call(place, images, cotangent, above, below, mine, other):
    rows, cols, width = images.shape
    shards, shard_rows, _ = mine.shape
    depth = shards * shard_rows
    ext = (rows + 2) * cols
    vmem = pl.BlockSpec(memory_space=pltpu.VMEM)
    return pl.pallas_call(
        block_body,
        out_shape=(
            jax.ShapeDtypeStruct(images.shape, BF16),
            jax.ShapeDtypeStruct(images.shape, BF16),
            jax.ShapeDtypeStruct(mine.shape, F32),
            jax.ShapeDtypeStruct(mine.shape, BF16),
        ),
        in_specs=[pl.BlockSpec(memory_space=pltpu.SMEM)] + [vmem] * 6,
        out_specs=(vmem,) * 4,
        scratch_shapes=[
            pltpu.VMEM((depth, width), F32),
            pltpu.VMEM((depth, width), F32),
            pltpu.VMEM((9 * width, width), BF16),
            pltpu.VMEM((9 * width, width), BF16),
            pltpu.VMEM((3, width, 3 * width), BF16),
            pltpu.VMEM((3, width, 3 * width), BF16),
            pltpu.VMEM(((rows + 4) * cols, 3 * width), BF16),
            pltpu.VMEM(((rows + 4) * cols, 3 * width), BF16),
            pltpu.VMEM((ext, 3 * width), BF16),
            pltpu.VMEM((ext, 3 * width), BF16),
            pltpu.VMEM((ext, width), F32),
            pltpu.VMEM((ext, width), F32),
            pltpu.VMEM((depth, width), F32),
            pltpu.VMEM((depth, width), F32),
        ],
        compiler_params=pltpu.CompilerParams(vmem_limit_bytes=48 * 1024 * 1024),
        cost_estimate=pl.CostEstimate(flops=4 * 10**9, bytes_accessed=4 * 10**6, transcendentals=0),
    )(place, images, cotangent, above, below, mine, other)


def per_device(images, cotangent, weight_one, weight_two):
    rows, cols = images.shape[1:3]
    dp, tiles = lax.axis_size("dp"), lax.axis_size("tile")
    device, tile = lax.axis_index("dp"), lax.axis_index("tile")
    core = device % 2
    swap = [(i, i ^ 1) for i in range(dp)]
    same_core = [list(range(c, dp, 2)) for c in range(2)]
    place = jnp.stack([core, tile == 0, tile == tiles - 1]).astype(jnp.int32)

    forward = [(i, i + 1) for i in range(tiles - 1)]
    backward = [(i + 1, i) for i in range(tiles - 1)]
    stacked = jnp.stack([images[0], cotangent[0]])
    above = lax.ppermute(stacked[:, rows - 2 :], "tile", forward)
    below = lax.ppermute(stacked[:, :2], "tile", backward)

    share = jnp.where(core == 0, weight_one, weight_two)
    copies = jnp.broadcast_to(share[None], (tiles, *share.shape))
    mine = lax.all_to_all(copies, "tile", 0, 0)
    other = lax.ppermute(mine, "dp", swap)

    out, image_grad, keep, send = block_call(place, images[0], cotangent[0], above, below, mine, other)

    pair = (keep + lax.ppermute(send, "dp", swap).astype(F32)).astype(BF16)
    parts = lax.all_to_all(pair, "tile", 0, 0)
    section = jnp.sum(parts.astype(F32), axis=0)
    copies = jnp.broadcast_to(section[None], (dp // 2, *section.shape))
    parts = lax.all_to_all(copies, "dp", 0, 0, axis_index_groups=same_core)
    scale = 1.0 / math.sqrt(dp * tiles * rows * cols)
    total = jnp.sum(parts, axis=0) * scale
    rest = lax.ppermute(total, "dp", swap)
    grad_one = jnp.where(core == 0, total, rest)
    grad_two = jnp.where(core == 0, rest, total)
    return out[None], image_grad[None], grad_one, grad_two


def solution(mesh):
    split, shard = P("dp", "tile", None, None), P("tile", None)
    return jax.shard_map(
        per_device,
        mesh=mesh,
        in_specs=(split, split, shard, shard),
        out_specs=(split, split, shard, shard),
        check_vma=False,
    )
```

```python
import math

import jax
import jax.numpy as jnp
from jax import lax
from jax.experimental import pallas as pl
from jax.experimental.pallas import tpu as pltpu
from jax.sharding import PartitionSpec as P

F32 = jnp.float32
BF16 = jnp.bfloat16


def dot(lhs, rhs, contract):
    return lax.dot_general(lhs, rhs, ((contract[:1], contract[1:]), ((), ())), preferred_element_type=F32)


VMEM = pl.BlockSpec(memory_space=pltpu.VMEM)


def call(body, outs, scratch, flops, limit, place, far, near, space=pl.ANY):
    moved = sum(math.prod(s.shape) * s.dtype.itemsize for s in (*outs, *far, *near))
    return pl.pallas_call(
        body,
        out_shape=tuple(outs),
        in_specs=[pl.BlockSpec(memory_space=pltpu.SMEM)] + [pl.BlockSpec(memory_space=space)] * len(far) + [VMEM] * len(near),
        out_specs=(VMEM,) * len(outs),
        scratch_shapes=[
            pltpu.SemaphoreType.DMA((len(far),)),
            *(pltpu.VMEM(s.shape, s.dtype) for s in far),
            *scratch,
        ],
        compiler_params=pltpu.CompilerParams(vmem_limit_bytes=limit * 1024 * 1024),
        cost_estimate=pl.CostEstimate(flops=flops, bytes_accessed=moved, transcendentals=0),
    )(place, *far, *near)


def fetch(sems, sources, targets):
    copies = [pltpu.make_async_copy(s, t, sems.at[i]) for i, (s, t) in enumerate(zip(sources, targets))]
    for copy in copies:
        copy.start()
    return copies


def put(shifts, row, value):
    cols, width = value.shape
    column = lax.broadcasted_iota(jnp.int32, (cols, width), 0)
    wide = value.astype(F32)
    at = pl.ds(row * cols, cols)
    low = jnp.where(column == 0, 0.0, pltpu.roll(wide, 1, 0))
    high = jnp.where(column == cols - 1, 0.0, pltpu.roll(wide, cols - 1, 0))
    shifts[at, 0:width] = low.astype(BF16)
    shifts[at, width : 2 * width] = value.astype(BF16)
    shifts[at, 2 * width : 3 * width] = high.astype(BF16)


def conv(shifts, down, count, cols):
    width = down.shape[1]
    total = None
    for a in range(3):
        part = dot(shifts[a * cols : (a + count) * cols, :], down[a * 3 * width : (a + 1) * 3 * width, :], (1, 0))
        total = part if total is None else total + part
    return total


def conv_back(shifts, across, count, cols):
    total = None
    for a in range(3):
        part = dot(shifts[(2 - a) * cols : (2 - a + count) * cols, :], across[a], (1, 1))
        total = part if total is None else total + part
    return total


def anchor_body(place, above, below, again):
    for i in range(again.shape[0]):
        again[i] = place[i]


def read_weights(place, mine, other, rows_one, rows_two):
    shards, shard_rows, _ = mine.shape
    first_core = place[0] == 0
    for shard in range(shards):
        slot = lax.rem(place[3] + shard, shards)
        own, rest = mine[slot].astype(F32), other[slot].astype(F32)
        at = pl.ds(shard * shard_rows, shard_rows)
        rows_one[at, :] = jnp.where(first_core, own, rest)
        rows_two[at, :] = jnp.where(first_core, rest, own)


def dense_taps(source):
    depth, width = source.shape[0] // 9, source.shape[1]
    line = lax.broadcasted_iota(jnp.int32, (width, width), 0) // depth
    lane = lax.broadcasted_iota(jnp.int32, (width, width), 1) // depth
    diagonal = line == lane
    for tap in range(9):
        piece = source[tap * depth : (tap + 1) * depth, :]
        yield tap, jnp.where(diagonal, jnp.concatenate([piece] * (width // depth), axis=0), 0.0).astype(BF16)


def fill_down(source, down):
    width = source.shape[1]
    for tap, dense in dense_taps(source):
        down[tap * width : (tap + 1) * width, :] = dense


def fill_across(source, across):
    width = source.shape[1]
    for tap, dense in dense_taps(source):
        a, b = divmod(tap, 3)
        across[a, :, (2 - b) * width : (3 - b) * width] = dense


def main_body(
    place, images_in, cotangent_in, above_in, below_in, mine, other,
    act_out, dpre_out, keep, send,
    sems, images, cotangent, above, below,
    rows_one, rows_two, down_one, across_two, x_shifts, g_shifts, dpre_shifts, pre, dact, sum_one, sum_two,
):
    rows, cols, width = images.shape
    shards, shard_rows, _ = mine.shape
    depth = shards * shard_rows // 9
    groups = width // depth
    first_core = place[0] == 0
    copies = fetch(sems, (images_in, cotangent_in, above_in, below_in), (images, cotangent, above, below))
    for copy in copies:
        copy.wait()
    for which, (shifts, block) in enumerate(((x_shifts, images), (g_shifts, cotangent))):
        for row in range(2):
            put(shifts, row, jnp.where(place[1] == 1, 0.0, above[which, row].astype(F32)))
            put(shifts, row + 2 + rows, jnp.where(place[2] == 1, 0.0, below[which, row].astype(F32)))
        for row in range(rows):
            put(shifts, row + 2, block[row])
    read_weights(place, mine, other, rows_one, rows_two)
    fill_down(rows_one, down_one)
    fill_across(rows_two, across_two)

    pre[...] = conv(x_shifts, down_one, rows + 2, cols)
    dact[...] = conv_back(g_shifts, across_two, rows + 2, cols)
    for row in range(rows + 2):
        at = pl.ds(row * cols, cols)
        value = pre[at, :]
        sig = jax.nn.sigmoid(value)
        act = value * sig
        dpre = dact[at, :] * (sig * (1.0 + value * (1.0 - sig)))
        if row in (0, rows + 1):
            outside = place[1 if row == 0 else 2] == 1
            act = jnp.where(outside, 0.0, act)
            dpre = jnp.where(outside, 0.0, dpre)
        act_out[at, :] = act.astype(BF16)
        dpre_out[at, :] = dpre.astype(BF16)
        if 0 < row < rows + 1:
            put(dpre_shifts, row - 1, dpre)

    def weight_sum(field, upstream, total):
        turned = field.T
        group = lax.broadcasted_iota(jnp.int32, (depth, width), 1) // depth
        for a in range(3):
            dense = dot(turned[:, a * cols : (a + rows) * cols], upstream, (1, 0))
            for j in range(3):
                piece = jnp.zeros((depth, width), F32)
                for g in range(groups):
                    block = dense[g * depth : (g + 1) * depth, j * width : (j + 1) * width]
                    piece = jnp.where(group == g, block, piece)
                tap = 3 * a + 2 - j
                total[tap * depth : (tap + 1) * depth, :] = piece

    weight_sum(x_shifts[cols : (rows + 3) * cols, width : 2 * width], dpre_shifts[...], sum_one)
    weight_sum(act_out[...], g_shifts[2 * cols : (rows + 2) * cols, :], sum_two)
    for shard in range(shards):
        at = pl.ds(shard * shard_rows, shard_rows)
        one, two = sum_one[at, :], sum_two[at, :]
        keep[shard] = jnp.where(first_core, one, two)
        send[shard] = jnp.where(first_core, two, one)


def last_body(
    place, images_in, cotangent_in, act_in, dpre_in, mine_in, other_in,
    out, image_grad,
    sems, images, cotangent, act, dpre, mine, other,
    rows_one, rows_two, down_two, across_one, act_shifts, dpre_shifts,
):
    rows, cols, _ = images.shape
    copies = fetch(
        sems,
        (images_in, cotangent_in, act_in, dpre_in, mine_in, other_in),
        (images, cotangent, act, dpre, mine, other),
    )
    for copy in copies:
        copy.wait()
    read_weights(place, mine, other, rows_one, rows_two)
    fill_down(rows_two, down_two)
    fill_across(rows_one, across_one)
    for row in range(rows + 2):
        put(act_shifts, row, act[row * cols : (row + 1) * cols, :])
        put(dpre_shifts, row, dpre[row * cols : (row + 1) * cols, :])
    total = conv(act_shifts, down_two, rows, cols)
    for row in range(rows):
        out[row] = (images[row].astype(F32) + total[row * cols : (row + 1) * cols, :]).astype(BF16)
    total = conv_back(dpre_shifts, across_one, rows, cols)
    for row in range(rows):
        image_grad[row] = (cotangent[row].astype(F32) + total[row * cols : (row + 1) * cols, :]).astype(BF16)


def per_device(images, cotangent, weight_one, weight_two):
    rows, cols = images.shape[1:3]
    dp, tiles = lax.axis_size("dp"), lax.axis_size("tile")
    device, tile = lax.axis_index("dp"), lax.axis_index("tile")
    core = device % 2
    swap = [(i, i ^ 1) for i in range(dp)]
    same_core = [list(range(c, dp, 2)) for c in range(2)]
    place = jnp.stack([core, tile == 0, tile == tiles - 1, jnp.zeros((), bool)]).astype(jnp.int32)

    def from_tile(value, step):
        return lax.ppermute(value, "tile", [((i + step) % tiles, i) for i in range(tiles)])

    stacked = jnp.stack([images[0], cotangent[0]])
    above, below = from_tile(stacked[:, rows - 2 :], -1), from_tile(stacked[:, :2], 1)
    share = jnp.where(core == 0, weight_one, weight_two)
    mine = lax.all_to_all(jnp.broadcast_to(share[None], (tiles, *share.shape)), "tile", 0, 0)

    shape = jax.ShapeDtypeStruct
    width = images.shape[3]
    full = tiles * weight_one.shape[0]
    dense = 9 * rows * cols * width * width * 2
    place = pl.pallas_call(
        anchor_body,
        out_shape=shape(place.shape, place.dtype),
        in_specs=[pl.BlockSpec(memory_space=pltpu.SMEM)] + [pl.BlockSpec(memory_space=pltpu.HBM)] * 2,
        out_specs=pl.BlockSpec(memory_space=pltpu.SMEM),
        compiler_params=pltpu.CompilerParams(vmem_limit_bytes=1024 * 1024),
        cost_estimate=pl.CostEstimate(flops=30 * dense, bytes_accessed=0, transcendentals=0),
    )(place, above, below)
    mine, place = lax.optimization_barrier((mine, place))
    other = lax.ppermute(mine, "dp", swap)
    outer = ((rows + 4) * cols, 3 * width)
    inner = ((rows + 2) * cols, 3 * width)
    plain = (inner[0], width)
    down, across = (9 * width, width), (3, width, 3 * width)
    act, dpre, keep, send = call(
        main_body,
        (shape(plain, BF16), shape(plain, BF16), shape(mine.shape, F32), shape(mine.shape, F32)),
        [
            pltpu.VMEM((full, width), F32),
            pltpu.VMEM((full, width), F32),
            pltpu.VMEM(down, BF16),
            pltpu.VMEM(across, BF16),
            pltpu.VMEM(outer, BF16),
            pltpu.VMEM(outer, BF16),
            pltpu.VMEM((rows * cols, 3 * width), BF16),
            pltpu.VMEM(plain, F32),
            pltpu.VMEM(plain, F32),
            pltpu.VMEM((full, width), F32),
            pltpu.VMEM((full, width), F32),
        ],
        5 * dense,
        24,
        place,
        (images[0], cotangent[0], above, below),
        (mine, other),
        pltpu.HBM,
    )
    pair = (keep + lax.ppermute(send, "dp", swap)).astype(BF16)
    block = shape(images.shape[1:], BF16)
    out, image_grad = call(
        last_body,
        (block, block),
        [
            pltpu.VMEM((full, width), F32),
            pltpu.VMEM((full, width), F32),
            pltpu.VMEM(down, BF16),
            pltpu.VMEM(across, BF16),
            pltpu.VMEM(inner, BF16),
            pltpu.VMEM(inner, BF16),
        ],
        4 * dense,
        16,
        place,
        (images[0], cotangent[0], act, dpre, mine, other),
        (),
    )
    parts = lax.all_to_all(pair, "tile", 0, 0)
    parts, out, image_grad = lax.optimization_barrier((parts, out, image_grad))
    section = jnp.sum(parts.astype(F32), axis=0)
    section = section.astype(BF16)
    copies = jnp.broadcast_to(section[None], (dp // 2, *section.shape))
    parts = lax.all_to_all(copies, "dp", 0, 0, axis_index_groups=same_core)
    scale = 1.0 / math.sqrt(dp * tiles * rows * cols)
    total = jnp.sum(parts.astype(F32), axis=0) * scale
    rest = lax.ppermute(total, "dp", swap)
    grad_one = jnp.where(core == 0, total, rest)
    grad_two = jnp.where(core == 0, rest, total)
    return out[None], image_grad[None], grad_one, grad_two


def solution(mesh):
    split, shard = P("dp", "tile", None, None), P("tile", None)
    return jax.shard_map(
        per_device,
        mesh=mesh,
        in_specs=(split, split, shard, shard),
        out_specs=(split, split, shard, shard),
        check_vma=False,
    )
```

```python
import math

import jax
import jax.numpy as jnp
from jax import lax
from jax.experimental import pallas as pl
from jax.experimental.pallas import tpu as pltpu
from jax.sharding import PartitionSpec as P

F32 = jnp.float32
BF16 = jnp.bfloat16


def dot(lhs, rhs, contract):
    return lax.dot_general(lhs, rhs, ((contract[:1], contract[1:]), ((), ())), preferred_element_type=F32)


VMEM = pl.BlockSpec(memory_space=pltpu.VMEM)


def in_hbm(array):
    return pltpu.with_memory_space_constraint(array, pltpu.HBM)


def call(body, outs, scratch, flops, limit, place, far, near, scalar_out=False, far_out=0):
    moved = sum(math.prod(s.shape) * s.dtype.itemsize for s in (*outs, *far, *near))
    return pl.pallas_call(
        body,
        out_shape=tuple(outs),
        in_specs=[pl.BlockSpec(memory_space=pltpu.SMEM)] + [pl.BlockSpec(memory_space=pl.ANY)] * len(far) + [VMEM] * len(near),
        out_specs=(pl.BlockSpec(memory_space=pltpu.HBM),) * far_out + (VMEM,) * (len(outs) - scalar_out - far_out) + (pl.BlockSpec(memory_space=pltpu.SMEM),) * scalar_out,
        scratch_shapes=[
            pltpu.SemaphoreType.DMA((max(len(far) + far_out, 1),)),
            *(pltpu.VMEM(s.shape, s.dtype) for s in far),
            *scratch,
        ],
        compiler_params=pltpu.CompilerParams(vmem_limit_bytes=limit * 1024 * 1024),
        cost_estimate=pl.CostEstimate(flops=flops, bytes_accessed=moved, transcendentals=0),
    )(place, *far, *near)


def fetch(sems, sources, targets):
    copies = [pltpu.make_async_copy(s, t, sems.at[i]) for i, (s, t) in enumerate(zip(sources, targets))]
    for copy in copies:
        copy.start()
    return copies


def put(shifts, row, value):
    cols, width = value.shape
    column = lax.broadcasted_iota(jnp.int32, (cols, width), 0)
    wide = value.astype(F32)
    at = pl.ds(row * cols, cols)
    low = jnp.where(column == 0, 0.0, pltpu.roll(wide, 1, 0))
    high = jnp.where(column == cols - 1, 0.0, pltpu.roll(wide, cols - 1, 0))
    shifts[at, 0:width] = low.astype(BF16)
    shifts[at, width : 2 * width] = value.astype(BF16)
    shifts[at, 2 * width : 3 * width] = high.astype(BF16)


def conv(shifts, down, count, cols):
    width = down.shape[1]
    total = None
    for a in range(3):
        part = dot(shifts[a * cols : (a + count) * cols, :], down[a * 3 * width : (a + 1) * 3 * width, :], (1, 0))
        total = part if total is None else total + part
    return total


def conv_back(shifts, across, count, cols):
    total = None
    for a in range(3):
        part = dot(shifts[(2 - a) * cols : (2 - a + count) * cols, :], across[a], (1, 1))
        total = part if total is None else total + part
    return total


def prepare_body(
    place, images_in, cotangent_in, above_in, below_in, x_shifts, g_shifts, again, sems, images, cotangent, above, below
):
    rows = images.shape[0]
    for i in range(again.shape[0]):
        again[i] = place[i]
    copies = fetch(sems, (images_in, cotangent_in, above_in, below_in), (images, cotangent, above, below))
    for copy in copies:
        copy.wait()
    for which, (shifts, block) in enumerate(((x_shifts, images), (g_shifts, cotangent))):
        put(shifts, 0, jnp.where(place[1] == 1, 0.0, above[which, 1].astype(F32)))
        for row in range(rows):
            put(shifts, row + 1, block[row])
        put(shifts, rows + 1, jnp.where(place[2] == 1, 0.0, below[which, 0].astype(F32)))


def pair_body(keep, received, out):
    shards, shard_rows, _ = out.shape
    for shard in range(shards):
        at = pl.ds(shard * shard_rows, shard_rows)
        out[shard] = (keep[at, :] + received[at, :]).astype(BF16)


def read_rows(shares, weight):
    shards, shard_rows, _ = shares.shape
    for shard in range(shards):
        weight[shard * shard_rows : (shard + 1) * shard_rows, :] = shares[shard].astype(F32)


def dense_taps(source):
    depth, width = source.shape[0] // 9, source.shape[1]
    line = lax.broadcasted_iota(jnp.int32, (width, width), 0) // depth
    lane = lax.broadcasted_iota(jnp.int32, (width, width), 1) // depth
    diagonal = line == lane
    for tap in range(9):
        piece = source[tap * depth : (tap + 1) * depth, :]
        yield tap, jnp.where(diagonal, jnp.concatenate([piece] * (width // depth), axis=0), 0.0).astype(BF16)


def fill_down(source, down):
    width = source.shape[1]
    for tap, dense in dense_taps(source):
        down[tap * width : (tap + 1) * width, :] = dense


def fill_across(source, across):
    width = source.shape[1]
    for tap, dense in dense_taps(source):
        a, b = divmod(tap, 3)
        across[a, :, (2 - b) * width : (3 - b) * width] = dense


def first_conv(one, shares, x_shifts, g_shifts, rows, cols, weight, down, across, result):
    read_rows(shares, weight)

    @pl.when(one)
    def _():
        fill_down(weight, down)
        result[...] = conv(x_shifts, down, rows, cols)

    @pl.when(jnp.logical_not(one))
    def _():
        fill_across(weight, across)
        result[...] = conv_back(g_shifts, across, rows, cols)


def early_body(place, mine, x_shifts, g_shifts, result, sems, weight, down, across):
    cols = (x_shifts.shape[0] - result.shape[0]) // 2
    first_conv(place[0] == 0, mine, x_shifts, g_shifts, result.shape[0] // cols, cols, weight, down, across, result)


def weight_sum(turned_of, upstream_of, total):
    depth, width = total.shape[0] // 9, total.shape[1]
    group = lax.broadcasted_iota(jnp.int32, (depth, width), 1) // depth
    for a in range(3):
        dense = dot(turned_of(a), upstream_of(a), (1, 0))
        for j in range(3):
            piece = jnp.zeros((depth, width), F32)
            for g in range(width // depth):
                block = dense[g * depth : (g + 1) * depth, j * width : (j + 1) * width]
                piece = jnp.where(group == g, block, piece)
            tap = 3 * a + 2 - j
            total[tap * depth : (tap + 1) * depth, :] = piece


def sum_one_of(x_shifts, dpre_shifts, cols, total):
    span, width = dpre_shifts.shape[0], total.shape[1]
    field = x_shifts[:, width : 2 * width].T
    weight_sum(lambda a: field[:, a * cols : a * cols + span], lambda a: dpre_shifts[...], total)


def sum_two_of(act, g_shifts, cols, total):
    span = act.shape[0]
    turned = act[...].T
    weight_sum(lambda a: turned, lambda a: g_shifts[(2 - a) * cols : (2 - a) * cols + span, :], total)


def main_body(
    place, early, other, x_shifts, g_shifts,
    act_out, dpre_out, act, dpre_shifts, send,
    sems, dpre, weight, down, across, late,
):
    cols = (x_shifts.shape[0] - early.shape[0]) // 2
    rows = early.shape[0] // cols
    first_core = place[0] == 0
    first_conv(jnp.logical_not(first_core), other, x_shifts, g_shifts, rows, cols, weight, down, across, late)
    for row in range(rows):
        at = pl.ds(row * cols, cols)
        value = jnp.where(first_core, early[at, :], late[at, :])
        dact = jnp.where(first_core, late[at, :], early[at, :])
        sig = jax.nn.sigmoid(value)
        act[at, :] = (value * sig).astype(BF16)
        slope = dact * (sig * (1.0 + value * (1.0 - sig)))
        dpre[at, :] = slope.astype(BF16)
        put(dpre_shifts, row, slope)
    copies = fetch(sems, (act, dpre), (act_out, dpre_out))

    @pl.when(first_core)
    def _():
        sum_two_of(act, g_shifts, cols, send)

    @pl.when(jnp.logical_not(first_core))
    def _():
        sum_one_of(x_shifts, dpre_shifts, cols, send)

    for copy in copies:
        copy.wait()


def keep_body(place, act, dpre_shifts, x_shifts, g_shifts, keep, sems):
    cols = (x_shifts.shape[0] - act.shape[0]) // 2

    @pl.when(place[0] == 0)
    def _():
        sum_one_of(x_shifts, dpre_shifts, cols, keep)

    @pl.when(place[0] != 0)
    def _():
        sum_two_of(act, g_shifts, cols, keep)


def last_body(
    place, images_in, cotangent_in, above_in, below_in, act_in, dpre_in, mine_in, other_in,
    out, image_grad,
    sems, images, cotangent, above, below, act, dpre, mine, other,
    rows_one, rows_two, down_one, across_two, down_two, across_one, x_edges, g_edges, act_shifts, dpre_shifts,
):
    rows, cols, _ = images.shape
    copies = fetch(
        sems,
        (images_in, cotangent_in, above_in, below_in, act_in, dpre_in, mine_in, other_in),
        (images, cotangent, above, below, act, dpre, mine, other),
    )
    for copy in copies:
        copy.wait()

    @pl.when(place[0] == 0)
    def _():
        read_rows(mine, rows_one)
        read_rows(other, rows_two)

    @pl.when(place[0] != 0)
    def _():
        read_rows(other, rows_one)
        read_rows(mine, rows_two)

    fill_down(rows_one, down_one)
    fill_down(rows_two, down_two)
    fill_across(rows_one, across_one)
    fill_across(rows_two, across_two)
    for row in range(rows):
        at = slice(row * cols, (row + 1) * cols)
        put(act_shifts, row + 1, act[at, :])
        put(dpre_shifts, row + 1, dpre[at, :])

    for which, (edges, block) in enumerate(((x_edges, images), (g_edges, cotangent))):
        for row in range(2):
            put(edges, row, jnp.where(place[1] == 1, 0.0, above[which, row].astype(F32)))
            put(edges, 4 + row, jnp.where(place[2] == 1, 0.0, below[which, row].astype(F32)))
        put(edges, 2, block[0])
        put(edges, 3, block[rows - 1])

    def at_edges(edges, step, weight_of, contract):
        total = None
        for a in range(3):
            row = a if step > 0 else 2 - a
            both = jnp.concatenate([edges[row * cols : (row + 1) * cols, :], edges[(row + 3) * cols : (row + 4) * cols, :]])
            part = dot(both, weight_of(a), contract)
            total = part if total is None else total + part
        return total

    span = 3 * images.shape[2]
    pre = at_edges(x_edges, 1, lambda a: down_one[a * span : (a + 1) * span, :], (1, 0))
    dact = at_edges(g_edges, -1, lambda a: across_two[a], (1, 1))
    sig = jax.nn.sigmoid(pre)
    act_edges = pre * sig
    dpre_edges = dact * (sig * (1.0 + pre * (1.0 - sig)))
    for shifts, edges in ((act_shifts, act_edges), (dpre_shifts, dpre_edges)):
        put(shifts, 0, jnp.where(place[1] == 1, 0.0, edges[:cols]))
        put(shifts, rows + 1, jnp.where(place[2] == 1, 0.0, edges[cols:]))

    total = conv(act_shifts, down_two, rows, cols)
    for row in range(rows):
        out[row] = (images[row].astype(F32) + total[row * cols : (row + 1) * cols, :]).astype(BF16)
    total = conv_back(dpre_shifts, across_one, rows, cols)
    for row in range(rows):
        image_grad[row] = (cotangent[row].astype(F32) + total[row * cols : (row + 1) * cols, :]).astype(BF16)


def per_device(images, cotangent, weight_one, weight_two):
    rows, cols = images.shape[1:3]
    dp, tiles = lax.axis_size("dp"), lax.axis_size("tile")
    device, tile = lax.axis_index("dp"), lax.axis_index("tile")
    core = device % 2
    swap = [(i, i ^ 1) for i in range(dp)]
    same_core = [list(range(c, dp, 2)) for c in range(2)]
    place = jnp.stack([core, tile == 0, tile == tiles - 1, jnp.zeros((), bool)]).astype(jnp.int32)

    def from_tile(value, step):
        return lax.ppermute(value, "tile", [((i + step) % tiles, i) for i in range(tiles)])

    shape = jax.ShapeDtypeStruct
    width = images.shape[3]
    first = jnp.stack([images[0, :2], cotangent[0, :2]])
    last_rows = jnp.stack([images[0, rows - 2 :], cotangent[0, rows - 2 :]])
    above, below = from_tile(last_rows, -1), from_tile(first, 1)
    share = jnp.where(core == 0, weight_one, weight_two)
    mine = lax.all_to_all(jnp.broadcast_to(share[None], (tiles, *share.shape)), "tile", 0, 0)

    full = tiles * weight_one.shape[0]
    dense = 9 * rows * cols * width * width * 2
    inner = ((rows + 2) * cols, 3 * width)
    plain = (rows * cols, width)
    down, across = (9 * width, width), (3, width, 3 * width)
    weight = pltpu.VMEM((full, width), F32)
    x_shifts, g_shifts, place = call(
        prepare_body,
        (shape(inner, BF16), shape(inner, BF16), shape(place.shape, place.dtype)),
        [],
        30 * dense,
        48,
        place,
        (in_hbm(images[0]), in_hbm(cotangent[0]), above, below),
        (),
        scalar_out=True,
    )
    mine, x_shifts, g_shifts, place = lax.optimization_barrier((mine, x_shifts, g_shifts, place))
    other = lax.ppermute(mine, "dp", swap)
    (early,) = call(
        early_body,
        (shape(plain, F32),),
        [weight, pltpu.VMEM(down, BF16), pltpu.VMEM(across, BF16)],
        dense,
        16,
        place,
        (),
        (mine, x_shifts, g_shifts),
    )
    near = shape(plain, BF16)
    half = shape((full, width), F32)
    act, dpre, act_near, dpre_shifts, send = call(
        main_body,
        (pltpu.HBM(plain, BF16), pltpu.HBM(plain, BF16), near, shape((rows * cols, 3 * width), BF16), half),
        [pltpu.VMEM(plain, BF16), weight, pltpu.VMEM(down, BF16), pltpu.VMEM(across, BF16), pltpu.VMEM(plain, F32)],
        3 * dense,
        16,
        place,
        (),
        (early, other, x_shifts, g_shifts),
        far_out=2,
    )
    received = lax.ppermute(send, "dp", swap)
    (keep,) = call(keep_body, (half,), [], 2 * dense, 16, place, (), (act_near, dpre_shifts, x_shifts, g_shifts))

    pair = pl.pallas_call(
        pair_body,
        out_shape=shape(mine.shape, BF16),
        in_specs=[VMEM] * 2,
        out_specs=VMEM,
        compiler_params=pltpu.CompilerParams(vmem_limit_bytes=4 * 1024 * 1024),
    )(keep, received)
    block = shape(images.shape[1:], BF16)
    out, image_grad = call(
        last_body,
        (block, block),
        [
            weight,
            weight,
            pltpu.VMEM(down, BF16),
            pltpu.VMEM(across, BF16),
            pltpu.VMEM(down, BF16),
            pltpu.VMEM(across, BF16),
            pltpu.VMEM((6 * cols, 3 * width), BF16),
            pltpu.VMEM((6 * cols, 3 * width), BF16),
            pltpu.VMEM(inner, BF16),
            pltpu.VMEM(inner, BF16),
        ],
        8 * dense,
        48,
        place,
        (*(in_hbm(array) for array in (images[0], cotangent[0], above, below, act, dpre)), mine, other),
        (),
    )
    parts = lax.all_to_all(pair, "tile", 0, 0)
    parts, out, image_grad = lax.optimization_barrier((parts, out, image_grad))
    section = jnp.sum(parts.astype(F32), axis=0)

    def from_part(value, step_x, step_y, step_core):
        ring = dp // 4
        pairs = []
        for i in range(dp):
            x, y, c = i // (2 * ring), i // 2 % ring, i % 2
            pairs.append((((x ^ step_x) * ring + (y + step_y) % ring) * 2 + (c ^ step_core), i))
        return lax.ppermute(value, "dp", pairs)

    after, before, across_ring = (from_part(section, 0, step, 0) for step in (1, dp // 4 - 1, dp // 8))
    section = (section + across_ring) + (after + before)
    section = section + from_part(section, 1, 0, 0)
    scale = 1.0 / math.sqrt(dp * tiles * rows * cols)
    total = section * scale
    rest = lax.ppermute(total, "dp", swap)
    grad_one = jnp.where(core == 0, total, rest)
    grad_two = jnp.where(core == 0, rest, total)
    return out[None], image_grad[None], grad_one, grad_two


def solution(mesh):
    split, shard = P("dp", "tile", None, None), P("tile", None)
    return jax.shard_map(
        per_device,
        mesh=mesh,
        in_specs=(split, split, shard, shard),
        out_specs=(split, split, shard, shard),
        check_vma=False,
    )
```

```python
import math

import jax
import jax.numpy as jnp
from jax import lax
from jax.experimental import pallas as pl
from jax.experimental.pallas import tpu as pltpu
from jax.sharding import PartitionSpec as P

F32 = jnp.float32
BF16 = jnp.bfloat16


def dot(lhs, rhs, contract):
    return lax.dot_general(lhs, rhs, ((contract[:1], contract[1:]), ((), ())), preferred_element_type=F32)


VMEM = pl.BlockSpec(memory_space=pltpu.VMEM)


def in_hbm(array):
    return pltpu.with_memory_space_constraint(array, pltpu.HBM)


def call(body, outs, scratch, flops, limit, place, far, near, scalar_out=False, far_out=0):
    moved = sum(math.prod(s.shape) * s.dtype.itemsize for s in (*outs, *far, *near))
    return pl.pallas_call(
        body,
        out_shape=tuple(outs),
        in_specs=[pl.BlockSpec(memory_space=pltpu.SMEM)] + [pl.BlockSpec(memory_space=pl.ANY)] * len(far) + [VMEM] * len(near),
        out_specs=(pl.BlockSpec(memory_space=pltpu.HBM),) * far_out + (VMEM,) * (len(outs) - scalar_out - far_out) + (pl.BlockSpec(memory_space=pltpu.SMEM),) * scalar_out,
        scratch_shapes=[
            pltpu.SemaphoreType.DMA((max(len(far) + far_out, 1),)),
            *(pltpu.VMEM(s.shape, s.dtype) for s in far),
            *scratch,
        ],
        compiler_params=pltpu.CompilerParams(vmem_limit_bytes=limit * 1024 * 1024),
        cost_estimate=pl.CostEstimate(flops=flops, bytes_accessed=moved, transcendentals=0),
    )(place, *far, *near)


def fetch(sems, sources, targets):
    copies = [pltpu.make_async_copy(s, t, sems.at[i]) for i, (s, t) in enumerate(zip(sources, targets))]
    for copy in copies:
        copy.start()
    return copies


def put(shifts, row, value):
    cols, width = value.shape
    column = lax.broadcasted_iota(jnp.int32, (cols, width), 0)
    wide = value.astype(F32)
    at = pl.ds(row * cols, cols)
    low = jnp.where(column == 0, 0.0, pltpu.roll(wide, 1, 0))
    high = jnp.where(column == cols - 1, 0.0, pltpu.roll(wide, cols - 1, 0))
    shifts[at, 0:width] = low.astype(BF16)
    shifts[at, width : 2 * width] = value.astype(BF16)
    shifts[at, 2 * width : 3 * width] = high.astype(BF16)


def conv(shifts, down, count, cols):
    width = down.shape[1]
    total = None
    for a in range(3):
        part = dot(shifts[a * cols : (a + count) * cols, :], down[a * 3 * width : (a + 1) * 3 * width, :], (1, 0))
        total = part if total is None else total + part
    return total


def conv_back(shifts, across, count, cols):
    total = None
    for a in range(3):
        part = dot(shifts[(2 - a) * cols : (2 - a + count) * cols, :], across[a], (1, 1))
        total = part if total is None else total + part
    return total


def prepare_body(
    place, images_in, cotangent_in, above_in, below_in, x_shifts, g_shifts, again, sems, images, cotangent, above, below
):
    rows = images.shape[0]
    for i in range(again.shape[0]):
        again[i] = place[i]
    copies = fetch(sems, (images_in, cotangent_in, above_in, below_in), (images, cotangent, above, below))
    for copy in copies:
        copy.wait()
    for which, (shifts, block) in enumerate(((x_shifts, images), (g_shifts, cotangent))):
        put(shifts, 0, jnp.where(place[1] == 1, 0.0, above[which, 1].astype(F32)))
        for row in range(rows):
            put(shifts, row + 1, block[row])
        put(shifts, rows + 1, jnp.where(place[2] == 1, 0.0, below[which, 0].astype(F32)))


def pair_body(keep, received, out):
    shards, shard_rows, _ = out.shape
    for shard in range(shards):
        at = pl.ds(shard * shard_rows, shard_rows)
        out[shard] = (keep[at, :] + received[at, :]).astype(BF16)


def read_rows(shares, weight):
    shards, shard_rows, _ = shares.shape
    for shard in range(shards):
        weight[shard * shard_rows : (shard + 1) * shard_rows, :] = shares[shard].astype(F32)


def dense_taps(source):
    depth, width = source.shape[0] // 9, source.shape[1]
    line = lax.broadcasted_iota(jnp.int32, (width, width), 0) // depth
    lane = lax.broadcasted_iota(jnp.int32, (width, width), 1) // depth
    diagonal = line == lane
    for tap in range(9):
        piece = source[tap * depth : (tap + 1) * depth, :]
        yield tap, jnp.where(diagonal, jnp.concatenate([piece] * (width // depth), axis=0), 0.0).astype(BF16)


def fill_down(source, down):
    width = source.shape[1]
    for tap, dense in dense_taps(source):
        down[tap * width : (tap + 1) * width, :] = dense


def fill_across(source, across):
    width = source.shape[1]
    for tap, dense in dense_taps(source):
        a, b = divmod(tap, 3)
        across[a, :, (2 - b) * width : (3 - b) * width] = dense


def first_conv(one, shares, x_shifts, g_shifts, rows, cols, weight, down, across, result):
    read_rows(shares, weight)

    @pl.when(one)
    def _():
        fill_down(weight, down)
        result[...] = conv(x_shifts, down, rows, cols)

    @pl.when(jnp.logical_not(one))
    def _():
        fill_across(weight, across)
        result[...] = conv_back(g_shifts, across, rows, cols)


def early_body(place, mine, x_shifts, g_shifts, result, sems, weight, down, across):
    cols = (x_shifts.shape[0] - result.shape[0]) // 2
    first_conv(place[0] == 0, mine, x_shifts, g_shifts, result.shape[0] // cols, cols, weight, down, across, result)


def weight_sum(turned_of, upstream_of, total):
    depth, width = total.shape[0] // 9, total.shape[1]
    group = lax.broadcasted_iota(jnp.int32, (depth, width), 1) // depth
    for a in range(3):
        dense = dot(turned_of(a), upstream_of(a), (1, 0))
        for j in range(3):
            piece = jnp.zeros((depth, width), F32)
            for g in range(width // depth):
                block = dense[g * depth : (g + 1) * depth, j * width : (j + 1) * width]
                piece = jnp.where(group == g, block, piece)
            tap = 3 * a + 2 - j
            total[tap * depth : (tap + 1) * depth, :] = piece


def sum_one_of(x_shifts, dpre_shifts, cols, total):
    span, width = dpre_shifts.shape[0], total.shape[1]
    field = x_shifts[:, width : 2 * width].T
    weight_sum(lambda a: field[:, a * cols : a * cols + span], lambda a: dpre_shifts[...], total)


def sum_two_of(act, g_shifts, cols, total):
    span = act.shape[0]
    turned = act[...].T
    weight_sum(lambda a: turned, lambda a: g_shifts[(2 - a) * cols : (2 - a) * cols + span, :], total)


def main_body(
    place, early, other, x_shifts, g_shifts,
    act_out, dpre_out, act, dpre_shifts, send,
    sems, dpre, weight, down, across, late,
):
    cols = (x_shifts.shape[0] - early.shape[0]) // 2
    rows = early.shape[0] // cols
    first_core = place[0] == 0
    first_conv(jnp.logical_not(first_core), other, x_shifts, g_shifts, rows, cols, weight, down, across, late)
    for row in range(rows):
        at = pl.ds(row * cols, cols)
        value = jnp.where(first_core, early[at, :], late[at, :])
        dact = jnp.where(first_core, late[at, :], early[at, :])
        sig = jax.nn.sigmoid(value)
        act[at, :] = (value * sig).astype(BF16)
        slope = dact * (sig * (1.0 + value * (1.0 - sig)))
        dpre[at, :] = slope.astype(BF16)
        put(dpre_shifts, row, slope)
    copies = fetch(sems, (act, dpre), (act_out, dpre_out))

    @pl.when(first_core)
    def _():
        sum_two_of(act, g_shifts, cols, send)

    @pl.when(jnp.logical_not(first_core))
    def _():
        sum_one_of(x_shifts, dpre_shifts, cols, send)

    for copy in copies:
        copy.wait()


def keep_body(place, act, dpre_shifts, x_shifts, g_shifts, keep, sems):
    cols = (x_shifts.shape[0] - act.shape[0]) // 2

    @pl.when(place[0] == 0)
    def _():
        sum_one_of(x_shifts, dpre_shifts, cols, keep)

    @pl.when(place[0] != 0)
    def _():
        sum_two_of(act, g_shifts, cols, keep)


def last_body(
    place, images_in, cotangent_in, above_in, below_in, act_in, dpre_in, mine, other,
    out, image_grad,
    sems, images, cotangent, above, below, act, dpre,
    rows_one, rows_two, down_one, across_two, down_two, across_one, x_edges, g_edges, act_shifts, dpre_shifts,
):
    rows, cols, _ = images.shape
    copies = fetch(
        sems,
        (images_in, cotangent_in, above_in, below_in, act_in, dpre_in),
        (images, cotangent, above, below, act, dpre),
    )
    for copy in copies:
        copy.wait()

    @pl.when(place[0] == 0)
    def _():
        read_rows(mine, rows_one)
        read_rows(other, rows_two)

    @pl.when(place[0] != 0)
    def _():
        read_rows(other, rows_one)
        read_rows(mine, rows_two)

    fill_down(rows_one, down_one)
    fill_down(rows_two, down_two)
    fill_across(rows_one, across_one)
    fill_across(rows_two, across_two)
    for row in range(rows):
        at = slice(row * cols, (row + 1) * cols)
        put(act_shifts, row + 1, act[at, :])
        put(dpre_shifts, row + 1, dpre[at, :])

    for which, (edges, block) in enumerate(((x_edges, images), (g_edges, cotangent))):
        for row in range(2):
            put(edges, row, jnp.where(place[1] == 1, 0.0, above[which, row].astype(F32)))
            put(edges, 4 + row, jnp.where(place[2] == 1, 0.0, below[which, row].astype(F32)))
        put(edges, 2, block[0])
        put(edges, 3, block[rows - 1])

    def at_edges(edges, step, weight_of, contract):
        total = None
        for a in range(3):
            row = a if step > 0 else 2 - a
            both = jnp.concatenate([edges[row * cols : (row + 1) * cols, :], edges[(row + 3) * cols : (row + 4) * cols, :]])
            part = dot(both, weight_of(a), contract)
            total = part if total is None else total + part
        return total

    span = 3 * images.shape[2]
    pre = at_edges(x_edges, 1, lambda a: down_one[a * span : (a + 1) * span, :], (1, 0))
    dact = at_edges(g_edges, -1, lambda a: across_two[a], (1, 1))
    sig = jax.nn.sigmoid(pre)
    act_edges = pre * sig
    dpre_edges = dact * (sig * (1.0 + pre * (1.0 - sig)))
    for shifts, edges in ((act_shifts, act_edges), (dpre_shifts, dpre_edges)):
        put(shifts, 0, jnp.where(place[1] == 1, 0.0, edges[:cols]))
        put(shifts, rows + 1, jnp.where(place[2] == 1, 0.0, edges[cols:]))

    total = conv(act_shifts, down_two, rows, cols)
    for row in range(rows):
        out[row] = (images[row].astype(F32) + total[row * cols : (row + 1) * cols, :]).astype(BF16)
    total = conv_back(dpre_shifts, across_one, rows, cols)
    for row in range(rows):
        image_grad[row] = (cotangent[row].astype(F32) + total[row * cols : (row + 1) * cols, :]).astype(BF16)


def per_device(images, cotangent, weight_one, weight_two):
    rows, cols = images.shape[1:3]
    dp, tiles = lax.axis_size("dp"), lax.axis_size("tile")
    device, tile = lax.axis_index("dp"), lax.axis_index("tile")
    core = device % 2
    swap = [(i, i ^ 1) for i in range(dp)]
    same_core = [list(range(c, dp, 2)) for c in range(2)]
    place = jnp.stack([core, tile == 0, tile == tiles - 1, jnp.zeros((), bool)]).astype(jnp.int32)

    def from_tile(value, step):
        return lax.ppermute(value, "tile", [((i + step) % tiles, i) for i in range(tiles)])

    shape = jax.ShapeDtypeStruct
    width = images.shape[3]
    first = jnp.stack([images[0, :2], cotangent[0, :2]])
    last_rows = jnp.stack([images[0, rows - 2 :], cotangent[0, rows - 2 :]])
    above, below = from_tile(last_rows, -1), from_tile(first, 1)
    share = jnp.where(core == 0, weight_one, weight_two)
    mine = lax.all_to_all(jnp.broadcast_to(share[None], (tiles, *share.shape)), "tile", 0, 0)

    full = tiles * weight_one.shape[0]
    dense = 9 * rows * cols * width * width * 2
    inner = ((rows + 2) * cols, 3 * width)
    plain = (rows * cols, width)
    down, across = (9 * width, width), (3, width, 3 * width)
    weight = pltpu.VMEM((full, width), F32)
    x_shifts, g_shifts, place = call(
        prepare_body,
        (shape(inner, BF16), shape(inner, BF16), shape(place.shape, place.dtype)),
        [],
        30 * dense,
        48,
        place,
        (in_hbm(images[0]), in_hbm(cotangent[0]), above, below),
        (),
        scalar_out=True,
    )
    mine, x_shifts, g_shifts, place = lax.optimization_barrier((mine, x_shifts, g_shifts, place))
    other = lax.ppermute(mine, "dp", swap)
    (early,) = call(
        early_body,
        (shape(plain, F32),),
        [weight, pltpu.VMEM(down, BF16), pltpu.VMEM(across, BF16)],
        dense,
        16,
        place,
        (),
        (mine, x_shifts, g_shifts),
    )
    near = shape(plain, BF16)
    half = shape((full, width), F32)
    act, dpre, act_near, dpre_shifts, send = call(
        main_body,
        (pltpu.HBM(plain, BF16), pltpu.HBM(plain, BF16), near, shape((rows * cols, 3 * width), BF16), half),
        [pltpu.VMEM(plain, BF16), weight, pltpu.VMEM(down, BF16), pltpu.VMEM(across, BF16), pltpu.VMEM(plain, F32)],
        3 * dense,
        16,
        place,
        (),
        (early, other, x_shifts, g_shifts),
        far_out=2,
    )
    received = lax.ppermute(send, "dp", swap)
    (keep,) = call(keep_body, (half,), [], 2 * dense, 16, place, (), (act_near, dpre_shifts, x_shifts, g_shifts))

    pair = pl.pallas_call(
        pair_body,
        out_shape=shape(mine.shape, BF16),
        in_specs=[VMEM] * 2,
        out_specs=VMEM,
        compiler_params=pltpu.CompilerParams(vmem_limit_bytes=4 * 1024 * 1024),
    )(keep, received)
    block = shape(images.shape[1:], BF16)
    out, image_grad = call(
        last_body,
        (block, block),
        [
            weight,
            weight,
            pltpu.VMEM(down, BF16),
            pltpu.VMEM(across, BF16),
            pltpu.VMEM(down, BF16),
            pltpu.VMEM(across, BF16),
            pltpu.VMEM((6 * cols, 3 * width), BF16),
            pltpu.VMEM((6 * cols, 3 * width), BF16),
            pltpu.VMEM(inner, BF16),
            pltpu.VMEM(inner, BF16),
        ],
        8 * dense,
        48,
        place,
        [in_hbm(array) for array in (images[0], cotangent[0], above, below, act, dpre)],
        (mine, other),
    )
    parts = lax.all_to_all(pair, "tile", 0, 0)
    parts, out, image_grad = lax.optimization_barrier((parts, out, image_grad))
    section = jnp.sum(parts.astype(F32), axis=0)

    def from_part(value, step_x, step_y, step_core):
        ring = dp // 4
        pairs = []
        for i in range(dp):
            x, y, c = i // (2 * ring), i // 2 % ring, i % 2
            pairs.append((((x ^ step_x) * ring + (y + step_y) % ring) * 2 + (c ^ step_core), i))
        return lax.ppermute(value, "dp", pairs)

    after, before, across_ring = (from_part(section, 0, step, 0) for step in (1, dp // 4 - 1, dp // 8))
    section = (section + across_ring) + (after + before)
    section = section + from_part(section, 1, 0, 0)
    scale = 1.0 / math.sqrt(dp * tiles * rows * cols)
    total = section * scale
    rest = lax.ppermute(total, "dp", swap)
    grad_one = jnp.where(core == 0, total, rest)
    grad_two = jnp.where(core == 0, rest, total)
    return out[None], image_grad[None], grad_one, grad_two


def solution(mesh):
    split, shard = P("dp", "tile", None, None), P("tile", None)
    return jax.shard_map(
        per_device,
        mesh=mesh,
        in_specs=(split, split, shard, shard),
        out_specs=(split, split, shard, shard),
        check_vma=False,
    )
```

```python
import math

import jax
import jax.numpy as jnp
from jax import lax
from jax.experimental import pallas as pl
from jax.experimental.pallas import tpu as pltpu
from jax.sharding import PartitionSpec as P

F32 = jnp.float32
BF16 = jnp.bfloat16


def dot(lhs, rhs, contract):
    return lax.dot_general(lhs, rhs, ((contract[:1], contract[1:]), ((), ())), preferred_element_type=F32)


VMEM = pl.BlockSpec(memory_space=pltpu.VMEM)


def in_hbm(array):
    return pltpu.with_memory_space_constraint(array, pltpu.HBM)


def call(body, outs, scratch, flops, limit, place, far, near, scalar_out=False, far_out=0):
    moved = sum(math.prod(s.shape) * s.dtype.itemsize for s in (*outs, *far, *near))
    return pl.pallas_call(
        body,
        out_shape=tuple(outs),
        in_specs=[pl.BlockSpec(memory_space=pltpu.SMEM)] + [pl.BlockSpec(memory_space=pl.ANY)] * len(far) + [VMEM] * len(near),
        out_specs=(pl.BlockSpec(memory_space=pltpu.HBM),) * far_out + (VMEM,) * (len(outs) - scalar_out - far_out) + (pl.BlockSpec(memory_space=pltpu.SMEM),) * scalar_out,
        scratch_shapes=[
            pltpu.SemaphoreType.DMA((max(len(far) + far_out, 1),)),
            *(pltpu.VMEM(s.shape, s.dtype) for s in far),
            *scratch,
        ],
        compiler_params=pltpu.CompilerParams(vmem_limit_bytes=limit * 1024 * 1024),
        cost_estimate=pl.CostEstimate(flops=flops, bytes_accessed=moved, transcendentals=0),
    )(place, *far, *near)


def fetch(sems, sources, targets):
    copies = [pltpu.make_async_copy(s, t, sems.at[i]) for i, (s, t) in enumerate(zip(sources, targets))]
    for copy in copies:
        copy.start()
    return copies


def put(shifts, row, value):
    cols, width = value.shape
    column = lax.broadcasted_iota(jnp.int32, (cols, width), 0)
    wide = value.astype(F32)
    at = pl.ds(row * cols, cols)
    low = jnp.where(column == 0, 0.0, pltpu.roll(wide, 1, 0))
    high = jnp.where(column == cols - 1, 0.0, pltpu.roll(wide, cols - 1, 0))
    shifts[at, 0:width] = low.astype(BF16)
    shifts[at, width : 2 * width] = value.astype(BF16)
    shifts[at, 2 * width : 3 * width] = high.astype(BF16)


def conv(shifts, down, count, cols):
    width = down.shape[1]
    total = None
    for a in range(3):
        part = dot(shifts[a * cols : (a + count) * cols, :], down[a * 3 * width : (a + 1) * 3 * width, :], (1, 0))
        total = part if total is None else total + part
    return total


def conv_back(shifts, across, count, cols):
    total = None
    for a in range(3):
        part = dot(shifts[(2 - a) * cols : (2 - a + count) * cols, :], across[a], (1, 1))
        total = part if total is None else total + part
    return total


def prepare_body(
    place, images_in, cotangent_in, above_in, below_in, x_shifts, g_shifts, again, sems, images, cotangent, above, below
):
    rows = images.shape[0]
    for i in range(again.shape[0]):
        again[i] = place[i]
    copies = fetch(sems, (images_in, cotangent_in, above_in, below_in), (images, cotangent, above, below))
    for copy in copies:
        copy.wait()
    for which, (shifts, block) in enumerate(((x_shifts, images), (g_shifts, cotangent))):
        put(shifts, 0, jnp.where(place[1] == 1, 0.0, above[which, 1].astype(F32)))
        for row in range(rows):
            put(shifts, row + 1, block[row])
        put(shifts, rows + 1, jnp.where(place[2] == 1, 0.0, below[which, 0].astype(F32)))


def pair_body(keep, received, out, both):
    shards, shard_rows, _ = out.shape
    both[...] = keep[...] + received[...].astype(F32)
    for shard in range(shards):
        at = pl.ds(shard * shard_rows, shard_rows)
        out[shard] = both[at, :].astype(BF16)


def read_rows(shares, weight):
    shards, shard_rows, _ = shares.shape
    for shard in range(shards):
        weight[shard * shard_rows : (shard + 1) * shard_rows, :] = shares[shard].astype(F32)


def dense_taps(source):
    depth, width = source.shape[0] // 9, source.shape[1]
    line = lax.broadcasted_iota(jnp.int32, (width, width), 0) // depth
    lane = lax.broadcasted_iota(jnp.int32, (width, width), 1) // depth
    diagonal = line == lane
    for tap in range(9):
        piece = source[tap * depth : (tap + 1) * depth, :]
        yield tap, jnp.where(diagonal, jnp.concatenate([piece] * (width // depth), axis=0), 0.0).astype(BF16)


def fill_down(source, down):
    width = source.shape[1]
    for tap, dense in dense_taps(source):
        down[tap * width : (tap + 1) * width, :] = dense


def fill_across(source, across):
    width = source.shape[1]
    for tap, dense in dense_taps(source):
        a, b = divmod(tap, 3)
        across[a, :, (2 - b) * width : (3 - b) * width] = dense


def first_conv(one, shares, x_shifts, g_shifts, rows, cols, weight, down, across, result):
    read_rows(shares, weight)

    @pl.when(one)
    def _():
        fill_down(weight, down)
        result[...] = conv(x_shifts, down, rows, cols)

    @pl.when(jnp.logical_not(one))
    def _():
        fill_across(weight, across)
        result[...] = conv_back(g_shifts, across, rows, cols)


def early_body(place, mine, x_shifts, g_shifts, result, sems, weight, down, across):
    cols = (x_shifts.shape[0] - result.shape[0]) // 2
    first_conv(place[0] == 0, mine, x_shifts, g_shifts, result.shape[0] // cols, cols, weight, down, across, result)


def weight_sum(turned_of, upstream_of, total):
    depth, width = total.shape[0] // 9, total.shape[1]
    group = lax.broadcasted_iota(jnp.int32, (depth, width), 1) // depth
    for a in range(3):
        dense = dot(turned_of(a), upstream_of(a), (1, 0))
        for j in range(3):
            piece = jnp.zeros((depth, width), F32)
            for g in range(width // depth):
                block = dense[g * depth : (g + 1) * depth, j * width : (j + 1) * width]
                piece = jnp.where(group == g, block, piece)
            tap = 3 * a + 2 - j
            total[tap * depth : (tap + 1) * depth, :] = piece.astype(total.dtype)


def sum_one_of(x_shifts, dpre_shifts, cols, total):
    span, width = dpre_shifts.shape[0], total.shape[1]
    field = x_shifts[:, width : 2 * width].T
    weight_sum(lambda a: field[:, a * cols : a * cols + span], lambda a: dpre_shifts[...], total)


def sum_two_of(act, g_shifts, cols, total):
    span = act.shape[0]
    turned = act[...].T
    weight_sum(lambda a: turned, lambda a: g_shifts[(2 - a) * cols : (2 - a) * cols + span, :], total)


def main_body(
    place, early, other, x_shifts, g_shifts,
    act_out, dpre_out, act, dpre_shifts, send,
    sems, dpre, weight, down, across, late,
):
    cols = (x_shifts.shape[0] - early.shape[0]) // 2
    rows = early.shape[0] // cols
    first_core = place[0] == 0
    first_conv(jnp.logical_not(first_core), other, x_shifts, g_shifts, rows, cols, weight, down, across, late)
    for row in range(rows):
        at = pl.ds(row * cols, cols)
        value = jnp.where(first_core, early[at, :], late[at, :])
        dact = jnp.where(first_core, late[at, :], early[at, :])
        sig = jax.nn.sigmoid(value)
        act[at, :] = (value * sig).astype(BF16)
        slope = dact * (sig * (1.0 + value * (1.0 - sig)))
        dpre[at, :] = slope.astype(BF16)
        put(dpre_shifts, row, slope)
    copies = fetch(sems, (act, dpre), (act_out, dpre_out))

    @pl.when(first_core)
    def _():
        sum_two_of(act, g_shifts, cols, send)

    @pl.when(jnp.logical_not(first_core))
    def _():
        sum_one_of(x_shifts, dpre_shifts, cols, send)

    for copy in copies:
        copy.wait()


def keep_body(place, act, dpre_shifts, x_shifts, g_shifts, keep, sems):
    cols = (x_shifts.shape[0] - act.shape[0]) // 2

    @pl.when(place[0] == 0)
    def _():
        sum_one_of(x_shifts, dpre_shifts, cols, keep)

    @pl.when(place[0] != 0)
    def _():
        sum_two_of(act, g_shifts, cols, keep)


def last_body(
    place, images_in, cotangent_in, above_in, below_in, act_in, dpre_in, mine, other,
    out, image_grad,
    sems, images, cotangent, above, below, act, dpre,
    rows_one, rows_two, down_one, across_two, down_two, across_one, x_edges, g_edges, act_shifts, dpre_shifts,
):
    rows, cols, _ = images.shape
    copies = fetch(
        sems,
        (images_in, cotangent_in, above_in, below_in, act_in, dpre_in),
        (images, cotangent, above, below, act, dpre),
    )
    for copy in copies:
        copy.wait()

    @pl.when(place[0] == 0)
    def _():
        read_rows(mine, rows_one)
        read_rows(other, rows_two)

    @pl.when(place[0] != 0)
    def _():
        read_rows(other, rows_one)
        read_rows(mine, rows_two)

    fill_down(rows_one, down_one)
    fill_down(rows_two, down_two)
    fill_across(rows_one, across_one)
    fill_across(rows_two, across_two)
    for row in range(rows):
        at = slice(row * cols, (row + 1) * cols)
        put(act_shifts, row + 1, act[at, :])
        put(dpre_shifts, row + 1, dpre[at, :])

    for which, (edges, block) in enumerate(((x_edges, images), (g_edges, cotangent))):
        for row in range(2):
            put(edges, row, jnp.where(place[1] == 1, 0.0, above[which, row].astype(F32)))
            put(edges, 4 + row, jnp.where(place[2] == 1, 0.0, below[which, row].astype(F32)))
        put(edges, 2, block[0])
        put(edges, 3, block[rows - 1])

    def at_edges(edges, step, weight_of, contract):
        total = None
        for a in range(3):
            row = a if step > 0 else 2 - a
            both = jnp.concatenate([edges[row * cols : (row + 1) * cols, :], edges[(row + 3) * cols : (row + 4) * cols, :]])
            part = dot(both, weight_of(a), contract)
            total = part if total is None else total + part
        return total

    span = 3 * images.shape[2]
    pre = at_edges(x_edges, 1, lambda a: down_one[a * span : (a + 1) * span, :], (1, 0))
    dact = at_edges(g_edges, -1, lambda a: across_two[a], (1, 1))
    sig = jax.nn.sigmoid(pre)
    act_edges = pre * sig
    dpre_edges = dact * (sig * (1.0 + pre * (1.0 - sig)))
    for shifts, edges in ((act_shifts, act_edges), (dpre_shifts, dpre_edges)):
        put(shifts, 0, jnp.where(place[1] == 1, 0.0, edges[:cols]))
        put(shifts, rows + 1, jnp.where(place[2] == 1, 0.0, edges[cols:]))

    total = conv(act_shifts, down_two, rows, cols)
    for row in range(rows):
        out[row] = (images[row].astype(F32) + total[row * cols : (row + 1) * cols, :]).astype(BF16)
    total = conv_back(dpre_shifts, across_one, rows, cols)
    for row in range(rows):
        image_grad[row] = (cotangent[row].astype(F32) + total[row * cols : (row + 1) * cols, :]).astype(BF16)


def per_device(images, cotangent, weight_one, weight_two):
    rows, cols = images.shape[1:3]
    dp, tiles = lax.axis_size("dp"), lax.axis_size("tile")
    device, tile = lax.axis_index("dp"), lax.axis_index("tile")
    core = device % 2
    swap = [(i, i ^ 1) for i in range(dp)]
    same_core = [list(range(c, dp, 2)) for c in range(2)]
    place = jnp.stack([core, tile == 0, tile == tiles - 1, jnp.zeros((), bool)]).astype(jnp.int32)

    def from_tile(value, step):
        return lax.ppermute(value, "tile", [((i + step) % tiles, i) for i in range(tiles)])

    shape = jax.ShapeDtypeStruct
    width = images.shape[3]
    first = jnp.stack([images[0, :2], cotangent[0, :2]])
    last_rows = jnp.stack([images[0, rows - 2 :], cotangent[0, rows - 2 :]])
    above, below = from_tile(last_rows, -1), from_tile(first, 1)
    share = jnp.where(core == 0, weight_one, weight_two)
    mine = lax.all_to_all(jnp.broadcast_to(share[None], (tiles, *share.shape)), "tile", 0, 0)

    full = tiles * weight_one.shape[0]
    dense = 9 * rows * cols * width * width * 2
    inner = ((rows + 2) * cols, 3 * width)
    plain = (rows * cols, width)
    down, across = (9 * width, width), (3, width, 3 * width)
    weight = pltpu.VMEM((full, width), F32)
    x_shifts, g_shifts, place = call(
        prepare_body,
        (shape(inner, BF16), shape(inner, BF16), shape(place.shape, place.dtype)),
        [],
        30 * dense,
        48,
        place,
        (in_hbm(images[0]), in_hbm(cotangent[0]), above, below),
        (),
        scalar_out=True,
    )
    mine, x_shifts, g_shifts, place = lax.optimization_barrier((mine, x_shifts, g_shifts, place))
    other = lax.ppermute(mine, "dp", swap)
    (early,) = call(
        early_body,
        (shape(plain, F32),),
        [weight, pltpu.VMEM(down, BF16), pltpu.VMEM(across, BF16)],
        dense,
        16,
        place,
        (),
        (mine, x_shifts, g_shifts),
    )
    near = shape(plain, BF16)
    half = shape((full, width), F32)
    act, dpre, act_near, dpre_shifts, send = call(
        main_body,
        (pltpu.HBM(plain, BF16), pltpu.HBM(plain, BF16), near, shape((rows * cols, 3 * width), BF16), shape((full, width), BF16)),
        [pltpu.VMEM(plain, BF16), weight, pltpu.VMEM(down, BF16), pltpu.VMEM(across, BF16), pltpu.VMEM(plain, F32)],
        3 * dense,
        16,
        place,
        (),
        (early, other, x_shifts, g_shifts),
        far_out=2,
    )
    received = lax.ppermute(send, "dp", swap)
    (keep,) = call(keep_body, (half,), [], 2 * dense, 16, place, (), (act_near, dpre_shifts, x_shifts, g_shifts))

    pair = pl.pallas_call(
        pair_body,
        out_shape=shape(mine.shape, BF16),
        in_specs=[VMEM] * 2,
        out_specs=VMEM,
        scratch_shapes=[weight],
        compiler_params=pltpu.CompilerParams(vmem_limit_bytes=4 * 1024 * 1024),
    )(keep, received)
    block = shape(images.shape[1:], BF16)
    out, image_grad = call(
        last_body,
        (block, block),
        [
            weight,
            weight,
            pltpu.VMEM(down, BF16),
            pltpu.VMEM(across, BF16),
            pltpu.VMEM(down, BF16),
            pltpu.VMEM(across, BF16),
            pltpu.VMEM((6 * cols, 3 * width), BF16),
            pltpu.VMEM((6 * cols, 3 * width), BF16),
            pltpu.VMEM(inner, BF16),
            pltpu.VMEM(inner, BF16),
        ],
        8 * dense,
        48,
        place,
        [in_hbm(array) for array in (images[0], cotangent[0], above, below, act, dpre)],
        (mine, other),
    )
    parts = lax.all_to_all(pair, "tile", 0, 0)
    parts, out, image_grad = lax.optimization_barrier((parts, out, image_grad))
    section = jnp.sum(parts.astype(F32), axis=0)

    def from_part(value, step_x, step_y, step_core):
        ring = dp // 4
        pairs = []
        for i in range(dp):
            x, y, c = i // (2 * ring), i // 2 % ring, i % 2
            pairs.append((((x ^ step_x) * ring + (y + step_y) % ring) * 2 + (c ^ step_core), i))
        return lax.ppermute(value, "dp", pairs)

    after, before, across_ring = (from_part(section, 0, step, 0) for step in (1, dp // 4 - 1, dp // 8))
    section = (section + across_ring) + (after + before)
    section = section + from_part(section, 1, 0, 0)
    scale = 1.0 / math.sqrt(dp * tiles * rows * cols)
    total = section * scale
    rest = lax.ppermute(total, "dp", swap)
    grad_one = jnp.where(core == 0, total, rest)
    grad_two = jnp.where(core == 0, rest, total)
    return out[None], image_grad[None], grad_one, grad_two


def solution(mesh):
    split, shard = P("dp", "tile", None, None), P("tile", None)
    return jax.shard_map(
        per_device,
        mesh=mesh,
        in_specs=(split, split, shard, shard),
        out_specs=(split, split, shard, shard),
        check_vma=False,
    )
```

```python
import math

import jax
import jax.numpy as jnp
from jax import lax
from jax.experimental import pallas as pl
from jax.experimental.pallas import tpu as pltpu
from jax.sharding import PartitionSpec as P

F32 = jnp.float32
BF16 = jnp.bfloat16


def dot(lhs, rhs, contract):
    return lax.dot_general(lhs, rhs, ((contract[:1], contract[1:]), ((), ())), preferred_element_type=F32)


VMEM = pl.BlockSpec(memory_space=pltpu.VMEM)


def in_hbm(array):
    return pltpu.with_memory_space_constraint(array, pltpu.HBM)


def call(body, outs, scratch, flops, limit, place, far, near, scalar_out=False, far_out=0):
    moved = sum(math.prod(s.shape) * s.dtype.itemsize for s in (*outs, *far, *near))
    return pl.pallas_call(
        body,
        out_shape=tuple(outs),
        in_specs=[pl.BlockSpec(memory_space=pltpu.SMEM)] + [pl.BlockSpec(memory_space=pl.ANY)] * len(far) + [VMEM] * len(near),
        out_specs=(pl.BlockSpec(memory_space=pltpu.HBM),) * far_out + (VMEM,) * (len(outs) - scalar_out - far_out) + (pl.BlockSpec(memory_space=pltpu.SMEM),) * scalar_out,
        scratch_shapes=[
            pltpu.SemaphoreType.DMA((max(len(far) + far_out, 1),)),
            *(pltpu.VMEM(s.shape, s.dtype) for s in far),
            *scratch,
        ],
        compiler_params=pltpu.CompilerParams(vmem_limit_bytes=limit * 1024 * 1024),
        cost_estimate=pl.CostEstimate(flops=flops, bytes_accessed=moved, transcendentals=0),
    )(place, *far, *near)


def fetch(sems, sources, targets):
    copies = [pltpu.make_async_copy(s, t, sems.at[i]) for i, (s, t) in enumerate(zip(sources, targets))]
    for copy in copies:
        copy.start()
    return copies


def put(shifts, row, value):
    cols, width = value.shape
    column = lax.broadcasted_iota(jnp.int32, (cols, width), 0)
    wide = value.astype(F32)
    at = pl.ds(row * cols, cols)
    low = jnp.where(column == 0, 0.0, pltpu.roll(wide, 1, 0))
    high = jnp.where(column == cols - 1, 0.0, pltpu.roll(wide, cols - 1, 0))
    shifts[at, 0:width] = low.astype(BF16)
    shifts[at, width : 2 * width] = value.astype(BF16)
    shifts[at, 2 * width : 3 * width] = high.astype(BF16)


def conv(shifts, down, count, cols):
    width = down.shape[1]
    total = None
    for a in range(3):
        part = dot(shifts[a * cols : (a + count) * cols, :], down[a * 3 * width : (a + 1) * 3 * width, :], (1, 0))
        total = part if total is None else total + part
    return total


def conv_back(shifts, across, count, cols):
    total = None
    for a in range(3):
        part = dot(shifts[(2 - a) * cols : (2 - a + count) * cols, :], across[a], (1, 1))
        total = part if total is None else total + part
    return total


def prepare_body(
    place, images_in, cotangent_in, above_in, below_in, x_shifts, g_shifts, again, sems, images, cotangent, above, below
):
    rows = images.shape[0]
    for i in range(again.shape[0]):
        again[i] = place[i]
    copies = fetch(sems, (images_in, cotangent_in, above_in, below_in), (images, cotangent, above, below))
    for copy in copies:
        copy.wait()
    for which, (shifts, block) in enumerate(((x_shifts, images), (g_shifts, cotangent))):
        put(shifts, 0, jnp.where(place[1] == 1, 0.0, above[which, 1].astype(F32)))
        for row in range(rows):
            put(shifts, row + 1, block[row])
        put(shifts, rows + 1, jnp.where(place[2] == 1, 0.0, below[which, 0].astype(F32)))


def pair_body(keep, received, out):
    shards, shard_rows, _ = out.shape
    for shard in range(shards):
        at = pl.ds(shard * shard_rows, shard_rows)
        out[shard] = (keep[at, :] + received[at, :]).astype(BF16)


def read_rows(shares, weight):
    shards, shard_rows, _ = shares.shape
    for shard in range(shards):
        weight[shard * shard_rows : (shard + 1) * shard_rows, :] = shares[shard].astype(F32)


def dense_taps(source):
    depth, width = source.shape[0] // 9, source.shape[1]
    line = lax.broadcasted_iota(jnp.int32, (width, width), 0) // depth
    lane = lax.broadcasted_iota(jnp.int32, (width, width), 1) // depth
    diagonal = line == lane
    for tap in range(9):
        piece = source[tap * depth : (tap + 1) * depth, :]
        yield tap, jnp.where(diagonal, jnp.concatenate([piece] * (width // depth), axis=0), 0.0).astype(BF16)


def fill_down(source, down):
    width = source.shape[1]
    for tap, dense in dense_taps(source):
        down[tap * width : (tap + 1) * width, :] = dense


def fill_across(source, across):
    width = source.shape[1]
    for tap, dense in dense_taps(source):
        a, b = divmod(tap, 3)
        across[a, :, (2 - b) * width : (3 - b) * width] = dense


def first_conv(one, shares, x_shifts, g_shifts, rows, cols, weight, down, across, result):
    read_rows(shares, weight)

    @pl.when(one)
    def _():
        fill_down(weight, down)
        result[...] = conv(x_shifts, down, rows, cols)

    @pl.when(jnp.logical_not(one))
    def _():
        fill_across(weight, across)
        result[...] = conv_back(g_shifts, across, rows, cols)


def early_body(place, mine, x_shifts, g_shifts, result, sems, weight, down, across):
    cols = (x_shifts.shape[0] - result.shape[0]) // 2
    first_conv(place[0] == 0, mine, x_shifts, g_shifts, result.shape[0] // cols, cols, weight, down, across, result)


def weight_sum(turned_of, upstream_of, total):
    depth, width = total.shape[0] // 9, total.shape[1]
    group = lax.broadcasted_iota(jnp.int32, (depth, width), 1) // depth
    for a in range(3):
        dense = dot(turned_of(a), upstream_of(a), (1, 0))
        for j in range(3):
            piece = jnp.zeros((depth, width), F32)
            for g in range(width // depth):
                block = dense[g * depth : (g + 1) * depth, j * width : (j + 1) * width]
                piece = jnp.where(group == g, block, piece)
            tap = 3 * a + 2 - j
            total[tap * depth : (tap + 1) * depth, :] = piece


def sum_one_of(x_shifts, dpre_shifts, cols, total):
    span, width = dpre_shifts.shape[0], total.shape[1]
    field = x_shifts[:, width : 2 * width].T
    weight_sum(lambda a: field[:, a * cols : a * cols + span], lambda a: dpre_shifts[...], total)


def sum_two_of(act, g_shifts, cols, total):
    span = act.shape[0]
    turned = act[...].T
    weight_sum(lambda a: turned, lambda a: g_shifts[(2 - a) * cols : (2 - a) * cols + span, :], total)


def main_body(
    place, early, other, x_shifts, g_shifts,
    act_out, dpre_out, act, dpre_shifts, send,
    sems, dpre, weight, down, across, late,
):
    cols = (x_shifts.shape[0] - early.shape[0]) // 2
    rows = early.shape[0] // cols
    first_core = place[0] == 0
    first_conv(jnp.logical_not(first_core), other, x_shifts, g_shifts, rows, cols, weight, down, across, late)
    for row in range(rows):
        at = pl.ds(row * cols, cols)
        value = jnp.where(first_core, early[at, :], late[at, :])
        dact = jnp.where(first_core, late[at, :], early[at, :])
        sig = jax.nn.sigmoid(value)
        act[at, :] = (value * sig).astype(BF16)
        slope = dact * (sig * (1.0 + value * (1.0 - sig)))
        dpre[at, :] = slope.astype(BF16)
        put(dpre_shifts, row, slope)
    copies = fetch(sems, (act, dpre), (act_out, dpre_out))

    @pl.when(first_core)
    def _():
        sum_two_of(act, g_shifts, cols, send)

    @pl.when(jnp.logical_not(first_core))
    def _():
        sum_one_of(x_shifts, dpre_shifts, cols, send)

    for copy in copies:
        copy.wait()


def keep_body(place, act, dpre_shifts, x_shifts, g_shifts, keep, sems):
    cols = (x_shifts.shape[0] - act.shape[0]) // 2

    @pl.when(place[0] == 0)
    def _():
        sum_one_of(x_shifts, dpre_shifts, cols, keep)

    @pl.when(place[0] != 0)
    def _():
        sum_two_of(act, g_shifts, cols, keep)


def last_body(
    place, images_in, cotangent_in, above_in, below_in, act_in, dpre_in, mine, other,
    out, image_grad,
    sems, images, cotangent, above, below, act, dpre,
    rows_one, rows_two, down_one, across_two, down_two, across_one, x_edges, g_edges, act_shifts, dpre_shifts,
):
    rows, cols, _ = images.shape
    copies = fetch(
        sems,
        (images_in, cotangent_in, above_in, below_in, act_in, dpre_in),
        (images, cotangent, above, below, act, dpre),
    )
    for copy in copies:
        copy.wait()

    @pl.when(place[0] == 0)
    def _():
        read_rows(mine, rows_one)
        read_rows(other, rows_two)

    @pl.when(place[0] != 0)
    def _():
        read_rows(other, rows_one)
        read_rows(mine, rows_two)

    fill_down(rows_one, down_one)
    fill_down(rows_two, down_two)
    fill_across(rows_one, across_one)
    fill_across(rows_two, across_two)
    for row in range(rows):
        at = slice(row * cols, (row + 1) * cols)
        put(act_shifts, row + 1, act[at, :])
        put(dpre_shifts, row + 1, dpre[at, :])

    for which, (edges, block) in enumerate(((x_edges, images), (g_edges, cotangent))):
        for row in range(2):
            put(edges, row, jnp.where(place[1] == 1, 0.0, above[which, row].astype(F32)))
            put(edges, 4 + row, jnp.where(place[2] == 1, 0.0, below[which, row].astype(F32)))
        put(edges, 2, block[0])
        put(edges, 3, block[rows - 1])

    def at_edges(edges, step, weight_of, contract):
        total = None
        for a in range(3):
            row = a if step > 0 else 2 - a
            both = jnp.concatenate([edges[row * cols : (row + 1) * cols, :], edges[(row + 3) * cols : (row + 4) * cols, :]])
            part = dot(both, weight_of(a), contract)
            total = part if total is None else total + part
        return total

    span = 3 * images.shape[2]
    pre = at_edges(x_edges, 1, lambda a: down_one[a * span : (a + 1) * span, :], (1, 0))
    dact = at_edges(g_edges, -1, lambda a: across_two[a], (1, 1))
    sig = jax.nn.sigmoid(pre)
    act_edges = pre * sig
    dpre_edges = dact * (sig * (1.0 + pre * (1.0 - sig)))
    for shifts, edges in ((act_shifts, act_edges), (dpre_shifts, dpre_edges)):
        put(shifts, 0, jnp.where(place[1] == 1, 0.0, edges[:cols]))
        put(shifts, rows + 1, jnp.where(place[2] == 1, 0.0, edges[cols:]))

    total = conv(act_shifts, down_two, rows, cols)
    for row in range(rows):
        out[row] = (images[row].astype(F32) + total[row * cols : (row + 1) * cols, :]).astype(BF16)
    total = conv_back(dpre_shifts, across_one, rows, cols)
    for row in range(rows):
        image_grad[row] = (cotangent[row].astype(F32) + total[row * cols : (row + 1) * cols, :]).astype(BF16)


def per_device(images, cotangent, weight_one, weight_two):
    rows, cols = images.shape[1:3]
    dp, tiles = lax.axis_size("dp"), lax.axis_size("tile")
    device, tile = lax.axis_index("dp"), lax.axis_index("tile")
    core = device % 2
    swap = [(i, i ^ 1) for i in range(dp)]
    same_core = [list(range(c, dp, 2)) for c in range(2)]
    place = jnp.stack([core, tile == 0, tile == tiles - 1, jnp.zeros((), bool)]).astype(jnp.int32)

    def from_tile(value, step):
        return lax.ppermute(value, "tile", [((i + step) % tiles, i) for i in range(tiles)])

    shape = jax.ShapeDtypeStruct
    width = images.shape[3]
    first = jnp.stack([images[0, :2], cotangent[0, :2]])
    last_rows = jnp.stack([images[0, rows - 2 :], cotangent[0, rows - 2 :]])
    above, below = from_tile(last_rows, -1), from_tile(first, 1)
    share = jnp.where(core == 0, weight_one, weight_two)
    mine = lax.all_to_all(jnp.broadcast_to(share[None], (tiles, *share.shape)), "tile", 0, 0)

    full = tiles * weight_one.shape[0]
    dense = 9 * rows * cols * width * width * 2
    inner = ((rows + 2) * cols, 3 * width)
    plain = (rows * cols, width)
    down, across = (9 * width, width), (3, width, 3 * width)
    weight = pltpu.VMEM((full, width), F32)
    x_shifts, g_shifts, place = call(
        prepare_body,
        (shape(inner, BF16), shape(inner, BF16), shape(place.shape, place.dtype)),
        [],
        30 * dense,
        48,
        place,
        (in_hbm(images[0]), in_hbm(cotangent[0]), above, below),
        (),
        scalar_out=True,
    )
    mine, x_shifts, g_shifts, place = lax.optimization_barrier((mine, x_shifts, g_shifts, place))
    other = lax.ppermute(mine, "dp", swap)
    (early,) = call(
        early_body,
        (shape(plain, F32),),
        [weight, pltpu.VMEM(down, BF16), pltpu.VMEM(across, BF16)],
        dense,
        16,
        place,
        (),
        (mine, x_shifts, g_shifts),
    )
    near = shape(plain, BF16)
    half = shape((full, width), F32)
    act, dpre, act_near, dpre_shifts, send = call(
        main_body,
        (pltpu.HBM(plain, BF16), pltpu.HBM(plain, BF16), near, shape((rows * cols, 3 * width), BF16), half),
        [pltpu.VMEM(plain, BF16), weight, pltpu.VMEM(down, BF16), pltpu.VMEM(across, BF16), pltpu.VMEM(plain, F32)],
        3 * dense,
        16,
        place,
        (),
        (early, other, x_shifts, g_shifts),
        far_out=2,
    )
    received = lax.ppermute(send, "dp", swap)
    (keep,) = call(keep_body, (half,), [], 2 * dense, 16, place, (), (act_near, dpre_shifts, x_shifts, g_shifts))

    pair = pl.pallas_call(
        pair_body,
        out_shape=shape(mine.shape, BF16),
        in_specs=[VMEM] * 2,
        out_specs=VMEM,
        compiler_params=pltpu.CompilerParams(vmem_limit_bytes=4 * 1024 * 1024),
    )(keep, received)
    block = shape(images.shape[1:], BF16)
    out, image_grad = call(
        last_body,
        (block, block),
        [
            weight,
            weight,
            pltpu.VMEM(down, BF16),
            pltpu.VMEM(across, BF16),
            pltpu.VMEM(down, BF16),
            pltpu.VMEM(across, BF16),
            pltpu.VMEM((6 * cols, 3 * width), BF16),
            pltpu.VMEM((6 * cols, 3 * width), BF16),
            pltpu.VMEM(inner, BF16),
            pltpu.VMEM(inner, BF16),
        ],
        8 * dense,
        48,
        place,
        [in_hbm(array) for array in (images[0], cotangent[0], above, below, act, dpre)],
        (mine, other),
    )
    parts = lax.all_to_all(pair, "tile", 0, 0)
    parts, out, image_grad = lax.optimization_barrier((parts, out, image_grad))
    section = jnp.sum(parts.astype(F32), axis=0)

    def from_part(value, step_x, step_y, step_core):
        ring = dp // 4
        pairs = []
        for i in range(dp):
            x, y, c = i // (2 * ring), i // 2 % ring, i % 2
            pairs.append((((x ^ step_x) * ring + (y + step_y) % ring) * 2 + (c ^ step_core), i))
        return lax.ppermute(value, "dp", pairs)

    section = section + from_part(section, 1, 0, 0)
    after, before, across_ring = (from_part(section, 0, step, 0) for step in (1, dp // 4 - 1, dp // 8))
    section = (section + across_ring) + (after + before)
    scale = 1.0 / math.sqrt(dp * tiles * rows * cols)
    total = section * scale
    rest = lax.ppermute(total, "dp", swap)
    grad_one = jnp.where(core == 0, total, rest)
    grad_two = jnp.where(core == 0, rest, total)
    return out[None], image_grad[None], grad_one, grad_two


def solution(mesh):
    split, shard = P("dp", "tile", None, None), P("tile", None)
    return jax.shard_map(
        per_device,
        mesh=mesh,
        in_specs=(split, split, shard, shard),
        out_specs=(split, split, shard, shard),
        check_vma=False,
    )
```

```python
import math

import jax
import jax.numpy as jnp
from jax import lax
from jax.experimental import pallas as pl
from jax.experimental.pallas import tpu as pltpu
from jax.sharding import PartitionSpec as P

F32 = jnp.float32
BF16 = jnp.bfloat16


def dot(lhs, rhs, contract):
    return lax.dot_general(lhs, rhs, ((contract[:1], contract[1:]), ((), ())), preferred_element_type=F32)


VMEM = pl.BlockSpec(memory_space=pltpu.VMEM)


def in_hbm(array):
    return pltpu.with_memory_space_constraint(array, pltpu.HBM)


def call(body, outs, scratch, flops, limit, place, far, near, scalar_out=False, far_out=0):
    moved = sum(math.prod(s.shape) * s.dtype.itemsize for s in (*outs, *far, *near))
    return pl.pallas_call(
        body,
        out_shape=tuple(outs),
        in_specs=[pl.BlockSpec(memory_space=pltpu.SMEM)] + [pl.BlockSpec(memory_space=pl.ANY)] * len(far) + [VMEM] * len(near),
        out_specs=(pl.BlockSpec(memory_space=pltpu.HBM),) * far_out + (VMEM,) * (len(outs) - scalar_out - far_out) + (pl.BlockSpec(memory_space=pltpu.SMEM),) * scalar_out,
        scratch_shapes=[
            pltpu.SemaphoreType.DMA((max(len(far) + far_out, 1),)),
            *(pltpu.VMEM(s.shape, s.dtype) for s in far),
            *scratch,
        ],
        compiler_params=pltpu.CompilerParams(vmem_limit_bytes=limit * 1024 * 1024),
        cost_estimate=pl.CostEstimate(flops=flops, bytes_accessed=moved, transcendentals=0),
    )(place, *far, *near)


def fetch(sems, sources, targets):
    copies = [pltpu.make_async_copy(s, t, sems.at[i]) for i, (s, t) in enumerate(zip(sources, targets))]
    for copy in copies:
        copy.start()
    return copies


def put(shifts, row, value):
    cols, width = value.shape
    column = lax.broadcasted_iota(jnp.int32, (cols, width), 0)
    wide = value.astype(F32)
    at = pl.ds(row * cols, cols)
    low = jnp.where(column == 0, 0.0, pltpu.roll(wide, 1, 0))
    high = jnp.where(column == cols - 1, 0.0, pltpu.roll(wide, cols - 1, 0))
    shifts[at, 0:width] = low.astype(BF16)
    shifts[at, width : 2 * width] = value.astype(BF16)
    shifts[at, 2 * width : 3 * width] = high.astype(BF16)


def conv(shifts, down, count, cols):
    width = down.shape[1]
    total = None
    for a in range(3):
        part = dot(shifts[a * cols : (a + count) * cols, :], down[a * 3 * width : (a + 1) * 3 * width, :], (1, 0))
        total = part if total is None else total + part
    return total


def conv_back(shifts, across, count, cols):
    total = None
    for a in range(3):
        part = dot(shifts[(2 - a) * cols : (2 - a + count) * cols, :], across[a], (1, 1))
        total = part if total is None else total + part
    return total


def prepare_body(
    place, images_in, cotangent_in, above_in, below_in, x_shifts, g_shifts, again, sems, images, cotangent, above, below
):
    rows = images.shape[0]
    for i in range(again.shape[0]):
        again[i] = place[i]
    copies = fetch(sems, (images_in, cotangent_in, above_in, below_in), (images, cotangent, above, below))
    for copy in copies:
        copy.wait()
    for which, (shifts, block) in enumerate(((x_shifts, images), (g_shifts, cotangent))):
        put(shifts, 0, jnp.where(place[1] == 1, 0.0, above[which, 1].astype(F32)))
        for row in range(rows):
            put(shifts, row + 1, block[row])
        put(shifts, rows + 1, jnp.where(place[2] == 1, 0.0, below[which, 0].astype(F32)))


def pair_body(keep, received, out):
    shards, shard_rows, _ = out.shape
    for shard in range(shards):
        at = pl.ds(shard * shard_rows, shard_rows)
        out[shard] = (keep[at, :] + received[at, :]).astype(BF16)


def read_rows(shares, weight):
    shards, shard_rows, _ = shares.shape
    for shard in range(shards):
        weight[shard * shard_rows : (shard + 1) * shard_rows, :] = shares[shard].astype(F32)


def dense_taps(source):
    depth, width = source.shape[0] // 9, source.shape[1]
    line = lax.broadcasted_iota(jnp.int32, (width, width), 0) // depth
    lane = lax.broadcasted_iota(jnp.int32, (width, width), 1) // depth
    diagonal = line == lane
    for tap in range(9):
        piece = source[tap * depth : (tap + 1) * depth, :]
        yield tap, jnp.where(diagonal, jnp.concatenate([piece] * (width // depth), axis=0), 0.0).astype(BF16)


def fill_down(source, down):
    width = source.shape[1]
    for tap, dense in dense_taps(source):
        down[tap * width : (tap + 1) * width, :] = dense


def fill_across(source, across):
    width = source.shape[1]
    for tap, dense in dense_taps(source):
        a, b = divmod(tap, 3)
        across[a, :, (2 - b) * width : (3 - b) * width] = dense


def first_conv(one, shares, x_shifts, g_shifts, rows, cols, weight, down, across, result):
    read_rows(shares, weight)

    @pl.when(one)
    def _():
        fill_down(weight, down)
        result[...] = conv(x_shifts, down, rows, cols)

    @pl.when(jnp.logical_not(one))
    def _():
        fill_across(weight, across)
        result[...] = conv_back(g_shifts, across, rows, cols)


def early_body(place, mine, x_shifts, g_shifts, result, sems, weight, down, across):
    cols = (x_shifts.shape[0] - result.shape[0]) // 2
    first_conv(place[0] == 0, mine, x_shifts, g_shifts, result.shape[0] // cols, cols, weight, down, across, result)


def weight_sum(turned_of, upstream_of, total):
    depth, width = total.shape[0] // 9, total.shape[1]
    group = lax.broadcasted_iota(jnp.int32, (depth, width), 1) // depth
    for a in range(3):
        dense = dot(turned_of(a), upstream_of(a), (1, 0))
        for j in range(3):
            piece = jnp.zeros((depth, width), F32)
            for g in range(width // depth):
                block = dense[g * depth : (g + 1) * depth, j * width : (j + 1) * width]
                piece = jnp.where(group == g, block, piece)
            tap = 3 * a + 2 - j
            total[tap * depth : (tap + 1) * depth, :] = piece


def sum_one_of(x_shifts, dpre_shifts, cols, total):
    span, width = dpre_shifts.shape[0], total.shape[1]
    field = x_shifts[:, width : 2 * width].T
    weight_sum(lambda a: field[:, a * cols : a * cols + span], lambda a: dpre_shifts[...], total)


def sum_two_of(act, g_shifts, cols, total):
    span = act.shape[0]
    turned = act[...].T
    weight_sum(lambda a: turned, lambda a: g_shifts[(2 - a) * cols : (2 - a) * cols + span, :], total)


def main_body(
    place, early, other, x_shifts, g_shifts,
    act_out, dpre_out, act, dpre_shifts, send,
    sems, dpre, weight, down, across, late,
):
    cols = (x_shifts.shape[0] - early.shape[0]) // 2
    rows = early.shape[0] // cols
    first_core = place[0] == 0
    first_conv(jnp.logical_not(first_core), other, x_shifts, g_shifts, rows, cols, weight, down, across, late)
    for row in range(rows):
        at = pl.ds(row * cols, cols)
        value = jnp.where(first_core, early[at, :], late[at, :])
        dact = jnp.where(first_core, late[at, :], early[at, :])
        sig = jax.nn.sigmoid(value)
        act[at, :] = (value * sig).astype(BF16)
        slope = dact * (sig * (1.0 + value * (1.0 - sig)))
        dpre[at, :] = slope.astype(BF16)
        put(dpre_shifts, row, slope)
    copies = fetch(sems, (act, dpre), (act_out, dpre_out))

    @pl.when(first_core)
    def _():
        sum_two_of(act, g_shifts, cols, send)

    @pl.when(jnp.logical_not(first_core))
    def _():
        sum_one_of(x_shifts, dpre_shifts, cols, send)

    for copy in copies:
        copy.wait()


def keep_body(place, act, dpre_shifts, x_shifts, g_shifts, keep, sems):
    cols = (x_shifts.shape[0] - act.shape[0]) // 2

    @pl.when(place[0] == 0)
    def _():
        sum_one_of(x_shifts, dpre_shifts, cols, keep)

    @pl.when(place[0] != 0)
    def _():
        sum_two_of(act, g_shifts, cols, keep)


def last_body(
    place, images_in, cotangent_in, above_in, below_in, act_in, dpre_in, mine, other,
    out, image_grad,
    sems, images, cotangent, above, below, act, dpre,
    rows_one, rows_two, down_one, across_two, down_two, across_one, x_edges, g_edges, act_shifts, dpre_shifts,
):
    rows, cols, _ = images.shape
    copies = fetch(
        sems,
        (images_in, cotangent_in, above_in, below_in, act_in, dpre_in),
        (images, cotangent, above, below, act, dpre),
    )
    for copy in copies:
        copy.wait()

    @pl.when(place[0] == 0)
    def _():
        read_rows(mine, rows_one)
        read_rows(other, rows_two)

    @pl.when(place[0] != 0)
    def _():
        read_rows(other, rows_one)
        read_rows(mine, rows_two)

    fill_down(rows_one, down_one)
    fill_down(rows_two, down_two)
    fill_across(rows_one, across_one)
    fill_across(rows_two, across_two)
    for row in range(rows):
        at = slice(row * cols, (row + 1) * cols)
        put(act_shifts, row + 1, act[at, :])
        put(dpre_shifts, row + 1, dpre[at, :])

    for which, (edges, block) in enumerate(((x_edges, images), (g_edges, cotangent))):
        for row in range(2):
            put(edges, row, jnp.where(place[1] == 1, 0.0, above[which, row].astype(F32)))
            put(edges, 4 + row, jnp.where(place[2] == 1, 0.0, below[which, row].astype(F32)))
        put(edges, 2, block[0])
        put(edges, 3, block[rows - 1])

    def at_edges(edges, step, weight_of, contract):
        total = None
        for a in range(3):
            row = a if step > 0 else 2 - a
            both = jnp.concatenate([edges[row * cols : (row + 1) * cols, :], edges[(row + 3) * cols : (row + 4) * cols, :]])
            part = dot(both, weight_of(a), contract)
            total = part if total is None else total + part
        return total

    span = 3 * images.shape[2]
    pre = at_edges(x_edges, 1, lambda a: down_one[a * span : (a + 1) * span, :], (1, 0))
    dact = at_edges(g_edges, -1, lambda a: across_two[a], (1, 1))
    sig = jax.nn.sigmoid(pre)
    act_edges = pre * sig
    dpre_edges = dact * (sig * (1.0 + pre * (1.0 - sig)))
    for shifts, edges in ((act_shifts, act_edges), (dpre_shifts, dpre_edges)):
        put(shifts, 0, jnp.where(place[1] == 1, 0.0, edges[:cols]))
        put(shifts, rows + 1, jnp.where(place[2] == 1, 0.0, edges[cols:]))

    total = conv(act_shifts, down_two, rows, cols)
    for row in range(rows):
        out[row] = (images[row].astype(F32) + total[row * cols : (row + 1) * cols, :]).astype(BF16)
    total = conv_back(dpre_shifts, across_one, rows, cols)
    for row in range(rows):
        image_grad[row] = (cotangent[row].astype(F32) + total[row * cols : (row + 1) * cols, :]).astype(BF16)


def per_device(images, cotangent, weight_one, weight_two):
    rows, cols = images.shape[1:3]
    dp, tiles = lax.axis_size("dp"), lax.axis_size("tile")
    device, tile = lax.axis_index("dp"), lax.axis_index("tile")
    core = device % 2
    swap = [(i, i ^ 1) for i in range(dp)]
    same_core = [list(range(c, dp, 2)) for c in range(2)]
    place = jnp.stack([core, tile == 0, tile == tiles - 1, jnp.zeros((), bool)]).astype(jnp.int32)

    def from_tile(value, step):
        return lax.ppermute(value, "tile", [((i + step) % tiles, i) for i in range(tiles)])

    shape = jax.ShapeDtypeStruct
    width = images.shape[3]
    first = jnp.stack([images[0, :2], cotangent[0, :2]])
    last_rows = jnp.stack([images[0, rows - 2 :], cotangent[0, rows - 2 :]])
    above, below = from_tile(last_rows, -1), from_tile(first, 1)
    share = jnp.where(core == 0, weight_one, weight_two)
    mine = lax.all_to_all(jnp.broadcast_to(share[None], (tiles, *share.shape)), "tile", 0, 0)

    full = tiles * weight_one.shape[0]
    dense = 9 * rows * cols * width * width * 2
    inner = ((rows + 2) * cols, 3 * width)
    plain = (rows * cols, width)
    down, across = (9 * width, width), (3, width, 3 * width)
    weight = pltpu.VMEM((full, width), F32)
    x_shifts, g_shifts, place = call(
        prepare_body,
        (shape(inner, BF16), shape(inner, BF16), shape(place.shape, place.dtype)),
        [],
        30 * dense,
        48,
        place,
        (in_hbm(images[0]), in_hbm(cotangent[0]), above, below),
        (),
        scalar_out=True,
    )
    mine, x_shifts, g_shifts, place = lax.optimization_barrier((mine, x_shifts, g_shifts, place))
    other = lax.ppermute(mine, "dp", swap)
    (early,) = call(
        early_body,
        (shape(plain, F32),),
        [weight, pltpu.VMEM(down, BF16), pltpu.VMEM(across, BF16)],
        dense,
        16,
        place,
        (),
        (mine, x_shifts, g_shifts),
    )
    near = shape(plain, BF16)
    half = shape((full, width), F32)
    act, dpre, act_near, dpre_shifts, send = call(
        main_body,
        (pltpu.HBM(plain, BF16), pltpu.HBM(plain, BF16), near, shape((rows * cols, 3 * width), BF16), half),
        [pltpu.VMEM(plain, BF16), weight, pltpu.VMEM(down, BF16), pltpu.VMEM(across, BF16), pltpu.VMEM(plain, F32)],
        3 * dense,
        16,
        place,
        (),
        (early, other, x_shifts, g_shifts),
        far_out=2,
    )
    received = lax.ppermute(send, "dp", swap)
    (keep,) = call(keep_body, (half,), [], 2 * dense, 16, place, (), (act_near, dpre_shifts, x_shifts, g_shifts))

    pair = pl.pallas_call(
        pair_body,
        out_shape=shape(mine.shape, BF16),
        in_specs=[VMEM] * 2,
        out_specs=VMEM,
        compiler_params=pltpu.CompilerParams(vmem_limit_bytes=4 * 1024 * 1024),
    )(keep, received)
    block = shape(images.shape[1:], BF16)
    out, image_grad = call(
        last_body,
        (block, block),
        [
            weight,
            weight,
            pltpu.VMEM(down, BF16),
            pltpu.VMEM(across, BF16),
            pltpu.VMEM(down, BF16),
            pltpu.VMEM(across, BF16),
            pltpu.VMEM((6 * cols, 3 * width), BF16),
            pltpu.VMEM((6 * cols, 3 * width), BF16),
            pltpu.VMEM(inner, BF16),
            pltpu.VMEM(inner, BF16),
        ],
        8 * dense,
        48,
        place,
        [in_hbm(array) for array in (images[0], cotangent[0], above, below, act, dpre)],
        (mine, other),
    )
    parts = lax.all_to_all(pair, "tile", 0, 0)
    parts, out, image_grad = lax.optimization_barrier((parts, out, image_grad))
    section = jnp.sum(parts.astype(F32), axis=0)

    def from_part(value, step_x, step_y, step_core):
        ring = dp // 4
        pairs = []
        for i in range(dp):
            x, y, c = i // (2 * ring), i // 2 % ring, i % 2
            pairs.append((((x ^ step_x) * ring + (y + step_y) % ring) * 2 + (c ^ step_core), i))
        return lax.ppermute(value, "dp", pairs)

    after, before, across_ring = (from_part(section, 0, step, 0) for step in (1, dp // 4 - 1, dp // 8))
    section = (section + across_ring) + (after + before)
    section = section * (1.0 / math.sqrt(dp * tiles * rows * cols))
    far, rest, far_rest = (from_part(section, x, 0, c) for x, c in ((1, 0), (0, 1), (1, 1)))
    total, rest = section + far, rest + far_rest
    grad_one = jnp.where(core == 0, total, rest)
    grad_two = jnp.where(core == 0, rest, total)
    return out[None], image_grad[None], grad_one, grad_two


def solution(mesh):
    split, shard = P("dp", "tile", None, None), P("tile", None)
    return jax.shard_map(
        per_device,
        mesh=mesh,
        in_specs=(split, split, shard, shard),
        out_specs=(split, split, shard, shard),
        check_vma=False,
    )
```
